32 devices in a mesh: dp: 4 (over y, x), seq: 8 (over z, core).
Axes of the slice: x: 2, y: 2, z: 4, core: 2. Of those that a mesh axis runs over, the one named last changes fastest.
Arguments:
- sequence: bfloat16 [16384, 1536], P(('dp', 'seq')), parts along dimension 0, may hold values from -6 to 6
- conv_weight: bfloat16 [5, 1536, 1536], replicated, may hold values from -0.0625 to 0.0625
- qkv_weight: bfloat16 [1536, 3072], P('seq'), may hold values from -2 to 2
- out_weight: bfloat16 [1024, 1536], P('seq'), may hold values from -4 to 4
Outputs:
- pooled: bfloat16 [8192, 1536], P(('dp', 'seq')), parts along dimension 0
- update: bfloat16 [8192, 1536], P(('dp', 'seq')), parts along dimension 0
The draws below stay inside these ranges and needn't reach their ends.
There are 4 independent parts, one for each index of `dp`. The reference program is written for one: setup_inputs(seed, part) draws one part's arguments, and reference() takes and returns one part's arrays. A program takes and returns all parts, laid end to end along the dimension named above; an argument that names none is the same for every part. Nothing has to cross between parts.
All inputs are finite; a program needn't handle non-finite values.
Results may differ from the reference program's by a relative error of at most 0.0065.
Values may be sent and summed in bfloat16 or wider, within the bound.
A program may use at most 128 MiB of HBM per device.

```python
import math
import jax
import jax.numpy as jnp
from jax import lax

D = 1536
HEADS = 8
HEAD_DIM = 128
WIDTH = 5
IN_POS = 4096


def draw_qkv_weight(key, part):
    key = jax.random.fold_in(key, 11)
    first, second, third = jax.random.split(key, 3)
    inner = HEADS * HEAD_DIM
    base = 1.4 * jax.random.normal(first, (D, inner), jnp.float32) / math.sqrt(D)
    other = 1.4 * jax.random.normal(second, (D, inner), jnp.float32) / math.sqrt(D)
    values = jax.random.normal(third, (D, inner), jnp.float32) / math.sqrt(D)
    queries = base
    keys = other
    whole = jnp.concatenate([queries, keys, values], axis=1)
    return jnp.clip(whole, -2.0, 2.0).astype(jnp.bfloat16)


def level_of(rng, dims, cuts, smallest, largest):
    factor_of = 1.0
    for position, parts in cuts:
        draws = jax.random.uniform(jax.random.fold_in(jax.random.fold_in(rng, 6), position), (parts,), jnp.float32, smallest / len(cuts), largest / len(cuts))
        factor_of = factor_of * jnp.repeat(jnp.exp(draws), dims[position] // parts).reshape((-1,) + (1,) * (len(dims) - 1 - position))
    return factor_of


def centred(rng, shape, scale, limit, cuts=(), kind=jnp.bfloat16):
    array = jax.random.normal(rng, shape, jnp.float32) * scale
    if len(cuts) > 0:
        array = level_of(rng, shape, cuts, -0.22, 0.18) * array
    return jnp.clip(array, min=-limit, max=limit).astype(kind)


def setup_inputs(seed: int = 0, part: int = 0) -> dict:
    key_of = jax.random.split(jax.random.key(seed), 5)
    part_splits = jax.random.split(jax.random.fold_in(key_of[4], part), 5)
    sequence = centred(part_splits[0], (IN_POS, D), 1.0, 6.0, ((0, 8),))
    conv_weight = centred(key_of[1], (WIDTH, D, D), (WIDTH * D) ** -0.5, 0.0625)
    qkv_weight = draw_qkv_weight(jax.random.fold_in(key_of[4], 71), part)
    out_weight = centred(key_of[3], (HEADS * HEAD_DIM, D), 0.25, 4.0, ((0, 8),))
    return {"sequence": sequence, "conv_weight": conv_weight, "qkv_weight": qkv_weight, "out_weight": out_weight}


def normalize(values):
    return values * lax.rsqrt(lax.optimization_barrier(jnp.mean(values * values, axis=-1, keepdims=True)) + 1e-06)

def reference(sequence, conv_weight, qkv_weight, out_weight):
    length = sequence.shape[0]
    inner = HEADS * HEAD_DIM
    source = sequence.astype(jnp.float32)
    activated = jax.nn.gelu(normalize(source)).astype(jnp.bfloat16)
    padded = jnp.pad(activated, ((2, 2), (0, 0)))
    mixed = source
    for offset in range(WIDTH):
        mixed = mixed + jnp.dot(padded[offset:offset + length], conv_weight[offset], preferred_element_type=jnp.float32)
    pooled = lax.optimization_barrier(jnp.max(mixed.reshape(length // 2, 2, -1), axis=1)).astype(jnp.bfloat16)
    count = pooled.shape[0]
    normed = normalize(pooled.astype(jnp.float32)).astype(jnp.bfloat16)
    projected = jnp.dot(normed, qkv_weight, preferred_element_type=jnp.float32).astype(jnp.bfloat16)
    queries = projected[:, :inner].reshape(count, HEADS, HEAD_DIM).transpose(1, 0, 2)
    keys = projected[:, inner:2 * inner].reshape(count, HEADS, HEAD_DIM).transpose(1, 0, 2)
    values = projected[:, 2 * inner:].reshape(count, HEADS, HEAD_DIM).transpose(1, 0, 2)
    factor = HEAD_DIM ** (-0.5)

    def one_head(triple):
        query_h, key_h, value_h = triple
        scores = jnp.dot(query_h, key_h.T, preferred_element_type=jnp.float32) * factor
        peak = lax.optimization_barrier(jnp.max(scores, axis=-1, keepdims=True))
        expo = jnp.exp(scores - peak)
        total = lax.optimization_barrier(jnp.sum(expo, axis=-1, keepdims=True))
        return jnp.dot(expo.astype(jnp.bfloat16), value_h, preferred_element_type=jnp.float32) / total
    heads_out = lax.map(one_head, (queries, keys, values))
    attended = heads_out.transpose(1, 0, 2).reshape(count, inner).astype(jnp.bfloat16)
    update = jnp.dot(attended, out_weight, preferred_element_type=jnp.float32).astype(jnp.bfloat16)
    return (pooled, update)
```

```python
import functools

import jax
import jax.numpy as jnp
from jax import lax
from jax.experimental import pallas as pl
from jax.experimental.pallas import tpu as pltpu
from jax.sharding import PartitionSpec as P

HEADS = 8
HEAD_DIM = 128
WIDTH = 5
MESH = pl.DeviceIdType.MESH
HALO = 16
MB = 1024 * 1024


def conv_kernel(count, seq_ref, w_ref, pooled_ref, low, high, wbuf, ebuf, obuf, taps, send_sem, recv_sem, w_sem):
    me = lax.axis_index("seq")
    half, wide = seq_ref.shape
    d = wide // 2
    step = wbuf.shape[2]
    chunks = d // step
    has_low = me > 0
    has_high = me < count - 1
    low_id = {"seq": lax.rem(me + count - 1, count)}
    high_id = {"seq": lax.rem(me + 1, count)}

    def w_copy(c):
        return pltpu.make_async_copy(w_ref.at[:, pl.ds(c * step, step)], wbuf.at[c], w_sem.at[c])

    for c in range(chunks):
        w_copy(c).start()

    barrier = pltpu.get_barrier_semaphore()

    for peer in (low_id, high_id):
        pl.semaphore_signal(barrier, inc=1, device_id=peer, device_id_type=MESH)
    pl.semaphore_wait(barrier, 2)

    up = pltpu.make_async_remote_copy(
        src_ref=seq_ref.at[pl.ds(half - HALO, HALO)], dst_ref=low,
        send_sem=send_sem.at[0], recv_sem=recv_sem.at[0], device_id=high_id, device_id_type=MESH)
    down = pltpu.make_async_remote_copy(
        src_ref=seq_ref.at[pl.ds(0, HALO)], dst_ref=high,
        send_sem=send_sem.at[1], recv_sem=recv_sem.at[1], device_id=low_id, device_id_type=MESH)

    @pl.when(has_high)
    def _():
        up.start()

    @pl.when(has_low)
    def _():
        down.start()

    def activate(rows):
        rows = rows.astype(jnp.float32)
        scale = lax.rsqrt(jnp.mean(rows * rows, axis=-1, keepdims=True) + 1e-06)
        return jax.nn.gelu(rows * scale)

    block = 32

    def act_step(i, _):
        r = pl.multiple_of(i * block, block)
        ebuf[pl.ds(r + 8, block), :] = activate(seq_ref[pl.ds(r, block), :d])
        obuf[pl.ds(r + 8, block), :] = activate(seq_ref[pl.ds(r, block), d:])
        return 0

    lax.fori_loop(0, half // block, act_step, 0)

    @pl.when(has_low)
    def _():
        down.wait_send()
        up.wait_recv()
        ebuf[0:8, :] = activate(low[:, :d])[8:16]
        obuf[0:8, :] = activate(low[:, d:])[8:16]

    @pl.when(jnp.logical_not(has_low))
    def _():
        ebuf[0:8, :] = jnp.zeros((8, d), jnp.float32)
        obuf[0:8, :] = jnp.zeros((8, d), jnp.float32)

    @pl.when(has_high)
    def _():
        up.wait_send()
        down.wait_recv()
        ebuf[half + 8 : half + 16, :] = activate(high[:, :d])[0:8]
        obuf[half + 8 : half + 16, :] = activate(high[:, d:])[0:8]

    @pl.when(jnp.logical_not(has_high))
    def _():
        ebuf[half + 8 : half + 16, :] = jnp.zeros((8, d), jnp.float32)
        obuf[half + 8 : half + 16, :] = jnp.zeros((8, d), jnp.float32)

    def place(c, _):
        k = pl.multiple_of(c * step, step)
        cols = pl.ds(k, step)

        def put(first, tap, value):
            taps[first : first + half, pl.ds(tap * d + k, step)] = value

        e_prev = ebuf[7 : 7 + half, cols].astype(jnp.bfloat16)
        e_here = ebuf[8 : 8 + half, cols].astype(jnp.bfloat16)
        e_next = ebuf[9 : 9 + half, cols].astype(jnp.bfloat16)
        put(0, 0, e_prev)
        put(0, 2, e_here)
        put(half, 1, e_here)
        put(0, 4, e_next)
        put(half, 3, e_next)
        o_prev = obuf[7 : 7 + half, cols].astype(jnp.bfloat16)
        o_here = obuf[8 : 8 + half, cols].astype(jnp.bfloat16)
        o_next = obuf[9 : 9 + half, cols].astype(jnp.bfloat16)
        put(0, 1, o_prev)
        put(half, 0, o_prev)
        put(0, 3, o_here)
        put(half, 2, o_here)
        put(half, 4, o_next)
        return 0

    lax.fori_loop(0, chunks, place, 0)

    def conv_step(c, _):
        w_copy(c).wait()
        k = pl.multiple_of(c * step, step)
        mixed = jnp.dot(taps[...], wbuf[c], preferred_element_type=jnp.float32)
        even = mixed[:half] + seq_ref[:, pl.ds(k, step)].astype(jnp.float32)
        odd = mixed[half:] + seq_ref[:, pl.ds(k + d, step)].astype(jnp.float32)
        pooled_ref[:, pl.ds(k, step)] = jnp.maximum(even, odd).astype(jnp.bfloat16)
        return 0

    lax.fori_loop(0, chunks, conv_step, 0)


def conv_pool(sequence, conv_weight, count):
    rows, d = sequence.shape
    half = rows // 2
    step = 256
    pairs = sequence.reshape(half, 2 * d)
    weight = conv_weight.reshape(WIDTH * d, d)
    return pl.pallas_call(
        functools.partial(conv_kernel, count),
        out_shape=jax.ShapeDtypeStruct((half, d), jnp.bfloat16),
        in_specs=[pl.BlockSpec(memory_space=pltpu.VMEM), pl.BlockSpec(memory_space=pl.ANY)],
        out_specs=pl.BlockSpec(memory_space=pltpu.VMEM),
        scratch_shapes=[
            pltpu.VMEM((HALO, 2 * d), jnp.bfloat16),
            pltpu.VMEM((HALO, 2 * d), jnp.bfloat16),
            pltpu.VMEM((d // step, WIDTH * d, step), jnp.bfloat16),
            pltpu.VMEM((half + 16, d), jnp.float32),
            pltpu.VMEM((half + 16, d), jnp.float32),
            pltpu.VMEM((rows, WIDTH * d), jnp.bfloat16),
            pltpu.SemaphoreType.DMA((2,)),
            pltpu.SemaphoreType.DMA((2,)),
            pltpu.SemaphoreType.DMA((d // step,)),
        ],
        compiler_params=pltpu.CompilerParams(
            collective_id=0, has_side_effects=True, vmem_limit_bytes=52 * MB),
        cost_estimate=pl.CostEstimate(
            flops=2 * rows * WIDTH * d * d, bytes_accessed=2 * WIDTH * d * d, transcendentals=rows * d),
        name="conv_pool",
    )(pairs, weight)


def attend_kernel(pooled_ref, w_ref, out_w_ref, update_ref, normed, wbuf, owbuf, send, recv, att_send, att_recv,
                  send_sem, recv_sem, asend_sem, arecv_sem, w_sem):
    me = lax.axis_index("seq")
    count, d = pooled_ref.shape
    inner = HEADS * HEAD_DIM

    def w_copy(t):
        return pltpu.make_async_copy(w_ref.at[:, pl.ds(t * inner, inner)], wbuf.at[t], w_sem.at[t])

    order = (1, 2, 0)
    for t in order:
        w_copy(t).start()
    ow_copy = pltpu.make_async_copy(out_w_ref, owbuf, w_sem.at[3])
    ow_copy.start()

    barrier = pltpu.get_barrier_semaphore()

    def greet(o, _):
        pl.semaphore_signal(
            barrier, inc=1, device_id={"seq": lax.rem(me + o, HEADS)}, device_id_type=MESH)
        return 0

    lax.fori_loop(1, HEADS, greet, 0)

    def norm_step(i, _):
        r = pl.multiple_of(i * 32, 32)
        rows = pooled_ref[pl.ds(r, 32), :].astype(jnp.float32)
        scale = lax.rsqrt(jnp.mean(rows * rows, axis=-1, keepdims=True) + 1e-06)
        normed[pl.ds(r, 32), :] = (rows * scale).astype(jnp.bfloat16)
        return 0

    lax.fori_loop(0, count // 32, norm_step, 0)
    pl.semaphore_wait(barrier, HEADS - 1)

    def piece(t, peer, slot):
        return pltpu.make_async_remote_copy(
            src_ref=send.at[t, peer], dst_ref=recv.at[t, slot],
            send_sem=send_sem.at[t, peer], recv_sem=recv_sem.at[t, slot],
            device_id={"seq": peer}, device_id_type=MESH)

    def back(peer, slot):
        return pltpu.make_async_remote_copy(
            src_ref=att_send.at[peer], dst_ref=att_recv.at[slot],
            send_sem=asend_sem.at[peer], recv_sem=arecv_sem.at[slot],
            device_id={"seq": peer}, device_id_type=MESH)

    for t in order:
        w_copy(t).wait()

        def project(p, _, t=t):
            k = pl.multiple_of(p * 256, 256)
            both = jnp.dot(
                normed[...], wbuf[t, :, pl.ds(k, 256)], preferred_element_type=jnp.float32
            ).astype(jnp.bfloat16)
            send[t, 2 * p] = both[:, :HEAD_DIM]
            send[t, 2 * p + 1] = both[:, HEAD_DIM:]
            return 0

        lax.fori_loop(0, HEADS // 2, project, 0)

        def post(o, _, t=t):
            piece(t, lax.rem(me + o, HEADS), me).start()
            return 0

        lax.fori_loop(1, HEADS, post, 0)
        recv[t, me] = send[t, me]

    def arrive(t):
        def one(o, _):
            source = lax.rem(me + HEADS - o, HEADS)
            piece(t, source, source).wait_recv()
            return 0

        lax.fori_loop(1, HEADS, one, 0)

    arrive(1)
    arrive(2)
    keys = recv.at[1]
    values = recv.at[2]
    factor = HEAD_DIM ** (-0.5) * 1.4426950408889634

    def attend(source):
        total_rows = HEADS * count
        raw = lax.dot_general(
            recv[0, source], keys[...].reshape(total_rows, HEAD_DIM),
            (((1,), (1,)), ((), ())), preferred_element_type=jnp.float32)
        peak = jnp.max(raw, axis=-1, keepdims=True)
        expo = jnp.exp2((raw - peak) * factor)
        total = jnp.sum(expo, axis=-1, keepdims=True)
        weighted = jnp.dot(
            expo.astype(jnp.bfloat16), values[...].reshape(total_rows, HEAD_DIM),
            preferred_element_type=jnp.float32)
        return (weighted / total).astype(jnp.bfloat16)

    def step(o, _):
        source = lax.rem(me + HEADS - o, HEADS)

        @pl.when(o > 0)
        def _():
            piece(0, source, source).wait_recv()

        att_send[source] = attend(source)

        @pl.when(o > 0)
        def _():
            back(source, me).start()

        return 0

    lax.fori_loop(0, HEADS, step, 0)
    att_recv[me] = att_send[me]

    def finish(o, _):
        peer = lax.rem(me + o, HEADS)
        for t in range(3):
            piece(t, peer, me).wait_send()
        back(peer, me).wait_send()
        back(peer, peer).wait_recv()
        return 0

    lax.fori_loop(1, HEADS, finish, 0)
    ow_copy.wait()
    joined = jnp.concatenate([att_recv[h] for h in range(HEADS)], axis=1)
    for p in range(d // 512):
        update_ref[:, p * 512 : (p + 1) * 512] = jnp.dot(
            joined, owbuf[:, p * 512 : (p + 1) * 512], preferred_element_type=jnp.float32
        ).astype(jnp.bfloat16)


def attention(pooled, qkv, out_weight):
    count, d = pooled.shape
    inner = HEADS * HEAD_DIM
    heads = (HEADS, count, HEAD_DIM)
    return pl.pallas_call(
        attend_kernel,
        out_shape=jax.ShapeDtypeStruct((count, d), jnp.bfloat16),
        in_specs=[
            pl.BlockSpec(memory_space=pltpu.VMEM),
            pl.BlockSpec(memory_space=pl.ANY),
            pl.BlockSpec(memory_space=pl.ANY),
        ],
        out_specs=pl.BlockSpec(memory_space=pltpu.VMEM),
        scratch_shapes=[
            pltpu.VMEM((count, d), jnp.bfloat16),
            pltpu.VMEM((3, d, inner), jnp.bfloat16),
            pltpu.VMEM((inner, d), jnp.bfloat16),
            pltpu.VMEM((3,) + heads, jnp.bfloat16),
            pltpu.VMEM((3,) + heads, jnp.bfloat16),
            pltpu.VMEM(heads, jnp.bfloat16),
            pltpu.VMEM(heads, jnp.bfloat16),
            pltpu.SemaphoreType.DMA((3, HEADS)),
            pltpu.SemaphoreType.DMA((3, HEADS)),
            pltpu.SemaphoreType.DMA((HEADS,)),
            pltpu.SemaphoreType.DMA((HEADS,)),
            pltpu.SemaphoreType.DMA((4,)),
        ],
        compiler_params=pltpu.CompilerParams(
            collective_id=1, has_side_effects=True, vmem_limit_bytes=44 * MB),
        cost_estimate=pl.CostEstimate(
            flops=2 * count * d * 4 * inner + 4 * count * HEADS * count * inner,
            bytes_accessed=8 * d * inner, transcendentals=count * count * HEADS * HEADS),
        name="attend",
    )(pooled, qkv, out_weight)


def normalize(values):
    return values * lax.rsqrt(jnp.mean(values * values, axis=-1, keepdims=True) + 1e-06)


def single_head(triple):
    query_rows, key_rows, value_rows = triple
    scores = jnp.dot(query_rows, key_rows.T, preferred_element_type=jnp.float32) * HEAD_DIM ** (
        -0.5
    )
    peak = jnp.max(scores, axis=-1, keepdims=True)
    expo = jnp.exp(scores - peak)
    total = jnp.sum(expo, axis=-1, keepdims=True)
    return (
        jnp.dot(expo.astype(jnp.bfloat16), value_rows, preferred_element_type=jnp.float32) / total
    ).astype(jnp.bfloat16)


def attention_groups(pooled, qkv_weight, out_weight):
    inner = HEADS * HEAD_DIM
    count = pooled.shape[0]
    normed = normalize(pooled.astype(jnp.float32)).astype(jnp.bfloat16)
    projected = jnp.dot(
        normed,
        lax.all_gather(qkv_weight, "seq", axis=0, tiled=True),
        preferred_element_type=jnp.float32,
    ).astype(jnp.bfloat16)
    seq_count = lax.axis_size("seq")
    groups = seq_count // HEADS
    share = count // groups
    query_send = (
        projected[:, :inner]
        .reshape(groups, share, HEADS, HEAD_DIM)
        .transpose(2, 0, 1, 3)
        .reshape(seq_count, share, HEAD_DIM)
    )
    pair_send = (
        projected[:, inner:]
        .reshape(count, 2, HEADS, HEAD_DIM)
        .transpose(2, 0, 1, 3)
        .reshape(HEADS, count, 2 * HEAD_DIM)
    )
    pair_send = jnp.repeat(pair_send, groups, axis=0)
    query_recv, pair_recv = (
        lax.all_to_all(query_send, "seq", split_axis=0, concat_axis=0, tiled=True),
        lax.all_to_all(pair_send, "seq", split_axis=0, concat_axis=0, tiled=True),
    )
    key_rows = pair_recv[:, :, :HEAD_DIM].reshape(seq_count * count, HEAD_DIM)
    value_rows = pair_recv[:, :, HEAD_DIM:].reshape(seq_count * count, HEAD_DIM)

    def per_source(query_rows):
        return single_head((query_rows, key_rows, value_rows))

    head_rows = lax.map(per_source, query_recv)
    returned = lax.all_to_all(head_rows, "seq", split_axis=0, concat_axis=0, tiled=True)
    attended = (
        returned.reshape(HEADS, groups, share, HEAD_DIM).transpose(1, 2, 0, 3).reshape(count, inner)
    )
    columns = attended
    update = jnp.dot(
        columns,
        lax.all_gather(out_weight, "seq", axis=0, tiled=True),
        preferred_element_type=jnp.float32,
    )
    return update.astype(jnp.bfloat16)


def on_device(sequence, conv_weight, qkv_weight, out_weight):
    count = lax.axis_size("seq")
    pooled = conv_pool(sequence, conv_weight, count)
    if count == HEADS:
        update = attention(
            pooled,
            lax.all_gather(qkv_weight, "seq", axis=0, tiled=True),
            lax.all_gather(out_weight, "seq", axis=0, tiled=True),
        )
    else:
        update = attention_groups(pooled, qkv_weight, out_weight)
    return (pooled, update)


def solution(mesh):
    return jax.shard_map(
        on_device,
        mesh=mesh,
        in_specs=(P(("dp", "seq"), None), P(), P("seq", None), P("seq", None)),
        out_specs=(P(("dp", "seq"), None), P(("dp", "seq"), None)),
        check_vma=False,
    )
```

```python
import functools

import jax
import jax.numpy as jnp
from jax import lax
from jax.experimental import pallas as pl
from jax.experimental.pallas import tpu as pltpu
from jax.sharding import PartitionSpec as P

HEADS = 8
HEAD_DIM = 128
WIDTH = 5
MESH = pl.DeviceIdType.MESH
HALO = 16
MB = 1024 * 1024
DP = 4
PAIRS = 4
REMOTE = 6


class Gather:
    def __init__(self, shard, whole, sems):
        self.shard, self.whole = shard, whole
        self.s1, self.r1, self.s2, self.r2, self.s3, self.r3, self.own_sem = sems
        self.me = lax.axis_index("seq")
        self.dp = lax.axis_index("dp")
        self.pair, self.core = self.me // 2, self.me % 2
        self.mate = self.pair * 2 + 1 - self.core
        self.width = whole.shape[2] // (2 * DP)

    def part(self, source, group, core):
        first = pl.multiple_of((2 * group + core) * self.width, 128)
        return self.whole.at[source, :, pl.ds(first, self.width)]

    def own(self):
        return pltpu.make_async_copy(self.shard, self.whole.at[self.me], self.own_sem.at[0])

    def to_mate(self):
        return pltpu.make_async_remote_copy(
            src_ref=self.shard, dst_ref=self.whole.at[self.me], send_sem=self.s1.at[self.mate],
            recv_sem=self.r1.at[self.me], device_id={"seq": self.mate}, device_id_type=MESH)

    def from_mate(self):
        return pltpu.make_async_remote_copy(
            src_ref=self.shard, dst_ref=self.whole.at[self.mate], send_sem=self.s1.at[self.me],
            recv_sem=self.r1.at[self.mate], device_id={"seq": self.mate}, device_id_type=MESH)

    def target(self, i):
        return ((self.pair + PAIRS - 1 - i // 2) % PAIRS) * 2 + i % 2

    def source(self, i):
        return ((self.pair + 1 + i // 2) % PAIRS) * 2 + i % 2

    def out1(self, i):
        peer = self.target(i)
        first = pl.multiple_of((2 * self.dp + peer % 2) * self.width, 128)
        return pltpu.make_async_remote_copy(
            src_ref=self.shard.at[:, pl.ds(first, self.width)], dst_ref=self.part(self.me, self.dp, peer % 2),
            send_sem=self.s1.at[peer], recv_sem=self.r1.at[self.me], device_id={"seq": peer}, device_id_type=MESH)

    def in1(self, i):
        source = self.source(i)
        block = self.part(source, self.dp, self.core)
        return pltpu.make_async_remote_copy(
            src_ref=block, dst_ref=block, send_sem=self.s1.at[source], recv_sem=self.r1.at[source],
            device_id={"seq": source}, device_id_type=MESH)

    def out2(self, i, j):
        source, peer = self.source(i), (self.dp + j) % DP
        block = self.part(source, self.dp, self.core)
        return pltpu.make_async_remote_copy(
            src_ref=block, dst_ref=block, send_sem=self.s2.at[source, peer], recv_sem=self.r2.at[source, self.dp],
            device_id={"dp": peer}, device_id_type=MESH)

    def in2(self, i, j):
        source, peer = self.source(i), (self.dp + j) % DP
        block = self.part(source, peer, self.core)
        return pltpu.make_async_remote_copy(
            src_ref=block, dst_ref=block, send_sem=self.s2.at[source, peer], recv_sem=self.r2.at[source, peer],
            device_id={"dp": peer}, device_id_type=MESH)

    def out3(self, i, group):
        source = self.source(i)
        block = self.part(source, group, self.core)
        return pltpu.make_async_remote_copy(
            src_ref=block, dst_ref=block, send_sem=self.s3.at[source, group], recv_sem=self.r3.at[source, group],
            device_id={"seq": self.mate}, device_id_type=MESH)

    def in3(self, i, group):
        source = self.source(i)
        block = self.part(source, group, 1 - self.core)
        return pltpu.make_async_remote_copy(
            src_ref=block, dst_ref=block, send_sem=self.s3.at[source, group], recv_sem=self.r3.at[source, group],
            device_id={"seq": self.mate}, device_id_type=MESH)

    def start(self):
        self.own().start()
        self.to_mate().start()

        def one(i, _):
            self.out1(i).start()
            return 0

        lax.fori_loop(0, REMOTE, one, 0)

    def relay(self, i):
        self.in1(i).wait_recv()
        for j in range(1, DP):
            self.out2(i, j).start()
        self.out3(i, self.dp).start()

    def finish(self):
        def second(i, _):
            for j in range(1, DP):
                self.in2(i, j).wait_recv()
                self.out3(i, (self.dp + j) % DP).start()
            return 0

        lax.fori_loop(0, REMOTE, second, 0)

        def last(i, _):
            self.out1(i).wait_send()
            for j in range(1, DP):
                self.out2(i, j).wait_send()
            for group in range(DP):
                self.out3(i, group).wait_send()
                self.in3(i, group).wait_recv()
            return 0

        lax.fori_loop(0, REMOTE, last, 0)
        self.own().wait()
        self.to_mate().wait_send()
        self.from_mate().wait_recv()


def conv_kernel(count, share, *refs):
    if share:
        seq_ref, w_ref, shard, pooled_ref, whole, *refs = refs
    else:
        seq_ref, w_ref, pooled_ref, *refs = refs
    low, high, wbuf, ebuf, obuf, taps, send_sem, recv_sem, w_sem, *sems = refs
    gather = Gather(shard, whole, sems) if share else None
    me = lax.axis_index("seq")
    half, wide = seq_ref.shape
    d = wide // 2
    step = wbuf.shape[2]
    chunks = d // step
    has_low = me > 0
    has_high = me < count - 1
    low_id = {"seq": lax.rem(me + count - 1, count)}
    high_id = {"seq": lax.rem(me + 1, count)}

    def w_copy(c):
        return pltpu.make_async_copy(w_ref.at[:, pl.ds(c * step, step)], wbuf.at[c], w_sem.at[c])

    for c in range(chunks):
        w_copy(c).start()

    barrier = pltpu.get_barrier_semaphore()

    if share:
        for o in range(1, count):
            pl.semaphore_signal(
                barrier, inc=1, device_id={"seq": lax.rem(me + o, count)}, device_id_type=MESH)
        for o in range(1, DP):
            pl.semaphore_signal(
                barrier, inc=1, device_id={"dp": (gather.dp + o) % DP}, device_id_type=MESH)
        pl.semaphore_wait(barrier, count + DP - 2)
    else:
        for peer in (low_id, high_id):
            pl.semaphore_signal(barrier, inc=1, device_id=peer, device_id_type=MESH)
        pl.semaphore_wait(barrier, 2)

    up = pltpu.make_async_remote_copy(
        src_ref=seq_ref.at[pl.ds(half - HALO, HALO)], dst_ref=low,
        send_sem=send_sem.at[0], recv_sem=recv_sem.at[0], device_id=high_id, device_id_type=MESH)
    down = pltpu.make_async_remote_copy(
        src_ref=seq_ref.at[pl.ds(0, HALO)], dst_ref=high,
        send_sem=send_sem.at[1], recv_sem=recv_sem.at[1], device_id=low_id, device_id_type=MESH)

    @pl.when(has_high)
    def _():
        up.start()

    @pl.when(has_low)
    def _():
        down.start()

    if share:
        gather.start()

    def activate(rows):
        rows = rows.astype(jnp.float32)
        scale = lax.rsqrt(jnp.mean(rows * rows, axis=-1, keepdims=True) + 1e-06)
        return jax.nn.gelu(rows * scale)

    block = 32

    def act_step(i, _):
        r = pl.multiple_of(i * block, block)
        ebuf[pl.ds(r + 8, block), :] = activate(seq_ref[pl.ds(r, block), :d])
        obuf[pl.ds(r + 8, block), :] = activate(seq_ref[pl.ds(r, block), d:])
        return 0

    lax.fori_loop(0, half // block, act_step, 0)

    @pl.when(has_low)
    def _():
        down.wait_send()
        up.wait_recv()
        ebuf[0:8, :] = activate(low[:, :d])[8:16]
        obuf[0:8, :] = activate(low[:, d:])[8:16]

    @pl.when(jnp.logical_not(has_low))
    def _():
        ebuf[0:8, :] = jnp.zeros((8, d), jnp.float32)
        obuf[0:8, :] = jnp.zeros((8, d), jnp.float32)

    @pl.when(has_high)
    def _():
        up.wait_send()
        down.wait_recv()
        ebuf[half + 8 : half + 16, :] = activate(high[:, :d])[0:8]
        obuf[half + 8 : half + 16, :] = activate(high[:, d:])[0:8]

    @pl.when(jnp.logical_not(has_high))
    def _():
        ebuf[half + 8 : half + 16, :] = jnp.zeros((8, d), jnp.float32)
        obuf[half + 8 : half + 16, :] = jnp.zeros((8, d), jnp.float32)

    def place(c, _):
        k = pl.multiple_of(c * step, step)
        cols = pl.ds(k, step)

        def put(first, tap, value):
            taps[first : first + half, pl.ds(tap * d + k, step)] = value

        e_prev = ebuf[7 : 7 + half, cols].astype(jnp.bfloat16)
        e_here = ebuf[8 : 8 + half, cols].astype(jnp.bfloat16)
        e_next = ebuf[9 : 9 + half, cols].astype(jnp.bfloat16)
        put(0, 0, e_prev)
        put(0, 2, e_here)
        put(half, 1, e_here)
        put(0, 4, e_next)
        put(half, 3, e_next)
        o_prev = obuf[7 : 7 + half, cols].astype(jnp.bfloat16)
        o_here = obuf[8 : 8 + half, cols].astype(jnp.bfloat16)
        o_next = obuf[9 : 9 + half, cols].astype(jnp.bfloat16)
        put(0, 1, o_prev)
        put(half, 0, o_prev)
        put(0, 3, o_here)
        put(half, 2, o_here)
        put(half, 4, o_next)
        return 0

    lax.fori_loop(0, chunks, place, 0)

    def conv_step(c, _):
        w_copy(c).wait()
        k = pl.multiple_of(c * step, step)
        mixed = jnp.dot(taps[...], wbuf[c], preferred_element_type=jnp.float32)
        even = mixed[:half] + seq_ref[:, pl.ds(k, step)].astype(jnp.float32)
        odd = mixed[half:] + seq_ref[:, pl.ds(k + d, step)].astype(jnp.float32)
        pooled_ref[:, pl.ds(k, step)] = jnp.maximum(even, odd).astype(jnp.bfloat16)
        if share:
            gather.relay(c)
        return 0

    lax.fori_loop(0, chunks, conv_step, 0)
    if share:
        gather.finish()


def conv_pool(sequence, conv_weight, count, shard=None):
    rows, d = sequence.shape
    half = rows // 2
    step = 256
    pairs = sequence.reshape(half, 2 * d)
    weight = conv_weight.reshape(WIDTH * d, d)
    share = shard is not None
    out_shape = jax.ShapeDtypeStruct((half, d), jnp.bfloat16)
    out_specs = pl.BlockSpec(memory_space=pltpu.VMEM)
    in_specs = [pl.BlockSpec(memory_space=pltpu.VMEM), pl.BlockSpec(memory_space=pl.ANY)]
    operands, sems = [pairs, weight], []
    if share:
        out_shape = (out_shape, jax.ShapeDtypeStruct((count,) + shard.shape, jnp.bfloat16))
        out_specs = (out_specs, pl.BlockSpec(memory_space=pl.ANY))
        in_specs.append(pl.BlockSpec(memory_space=pl.ANY))
        operands.append(shard)
        sems = [pltpu.SemaphoreType.DMA((count,))] * 2 + [pltpu.SemaphoreType.DMA((count, DP))] * 4
        sems.append(pltpu.SemaphoreType.DMA((1,)))
    return pl.pallas_call(
        functools.partial(conv_kernel, count, share),
        out_shape=out_shape,
        in_specs=in_specs,
        out_specs=out_specs,
        scratch_shapes=[
            pltpu.VMEM((HALO, 2 * d), jnp.bfloat16),
            pltpu.VMEM((HALO, 2 * d), jnp.bfloat16),
            pltpu.VMEM((d // step, WIDTH * d, step), jnp.bfloat16),
            pltpu.VMEM((half + 16, d), jnp.float32),
            pltpu.VMEM((half + 16, d), jnp.float32),
            pltpu.VMEM((rows, WIDTH * d), jnp.bfloat16),
            pltpu.SemaphoreType.DMA((2,)),
            pltpu.SemaphoreType.DMA((2,)),
            pltpu.SemaphoreType.DMA((d // step,)),
        ] + sems,
        compiler_params=pltpu.CompilerParams(
            collective_id=0, has_side_effects=True, vmem_limit_bytes=52 * MB),
        cost_estimate=pl.CostEstimate(
            flops=2 * rows * WIDTH * d * d, bytes_accessed=2 * WIDTH * d * d, transcendentals=rows * d),
        name="conv_pool",
    )(*operands)


def attend_kernel(pooled_ref, w_ref, update_ref, normed, wbuf, owbuf, send, recv, att_send, att_recv,
                  send_sem, recv_sem, asend_sem, arecv_sem, w_sem):
    me = lax.axis_index("seq")
    count, d = pooled_ref.shape
    inner = HEADS * HEAD_DIM
    depth = d // HEADS

    def w_copy(t):
        return pltpu.make_async_copy(
            w_ref.at[:, pl.ds(0, depth), pl.ds(t * inner, inner)], wbuf.at[t], w_sem.at[t])

    def ow_copy(part):
        return pltpu.make_async_copy(
            w_ref.at[:, pl.ds(depth, HEAD_DIM // 2), pl.ds(part * d, d)], owbuf.at[:, part], w_sem.at[3 + part])

    order = (1, 2, 0)
    for t in order:
        w_copy(t).start()
    for part in range(2):
        ow_copy(part).start()

    barrier = pltpu.get_barrier_semaphore()

    def greet(o, _):
        pl.semaphore_signal(
            barrier, inc=1, device_id={"seq": lax.rem(me + o, HEADS)}, device_id_type=MESH)
        return 0

    lax.fori_loop(1, HEADS, greet, 0)

    def norm_step(i, _):
        r = pl.multiple_of(i * 32, 32)
        rows = pooled_ref[pl.ds(r, 32), :].astype(jnp.float32)
        scale = lax.rsqrt(jnp.mean(rows * rows, axis=-1, keepdims=True) + 1e-06)
        normed[pl.ds(r, 32), :] = (rows * scale).astype(jnp.bfloat16)
        return 0

    lax.fori_loop(0, count // 32, norm_step, 0)
    pl.semaphore_wait(barrier, HEADS - 1)

    def piece(t, peer, slot):
        return pltpu.make_async_remote_copy(
            src_ref=send.at[t, peer], dst_ref=recv.at[t, slot],
            send_sem=send_sem.at[t, peer], recv_sem=recv_sem.at[t, slot],
            device_id={"seq": peer}, device_id_type=MESH)

    def back(peer, slot):
        return pltpu.make_async_remote_copy(
            src_ref=att_send.at[peer], dst_ref=att_recv.at[slot],
            send_sem=asend_sem.at[peer], recv_sem=arecv_sem.at[slot],
            device_id={"seq": peer}, device_id_type=MESH)

    for t in order:
        w_copy(t).wait()

        def project(p, _, t=t):
            k = pl.multiple_of(p * 256, 256)
            both = jnp.dot(
                normed[...], wbuf[t, :, :, pl.ds(k, 256)].reshape(d, 256), preferred_element_type=jnp.float32
            ).astype(jnp.bfloat16)
            send[t, 2 * p] = both[:, :HEAD_DIM]
            send[t, 2 * p + 1] = both[:, HEAD_DIM:]
            return 0

        lax.fori_loop(0, HEADS // 2, project, 0)

        def post(o, _, t=t):
            piece(t, lax.rem(me + o, HEADS), me).start()
            return 0

        lax.fori_loop(1, HEADS, post, 0)
        recv[t, me] = send[t, me]

    def arrive(t):
        def one(o, _):
            source = lax.rem(me + HEADS - o, HEADS)
            piece(t, source, source).wait_recv()
            return 0

        lax.fori_loop(1, HEADS, one, 0)

    arrive(1)
    arrive(2)
    keys = recv.at[1]
    values = recv.at[2]
    factor = HEAD_DIM ** (-0.5) * 1.4426950408889634

    def attend(source):
        total_rows = HEADS * count
        raw = lax.dot_general(
            recv[0, source], keys[...].reshape(total_rows, HEAD_DIM),
            (((1,), (1,)), ((), ())), preferred_element_type=jnp.float32)
        peak = jnp.max(raw, axis=-1, keepdims=True)
        expo = jnp.exp2((raw - peak) * factor)
        total = jnp.sum(expo, axis=-1, keepdims=True)
        weighted = jnp.dot(
            expo.astype(jnp.bfloat16), values[...].reshape(total_rows, HEAD_DIM),
            preferred_element_type=jnp.float32)
        return (weighted / total).astype(jnp.bfloat16)

    def step(o, _):
        source = lax.rem(me + HEADS - o, HEADS)

        @pl.when(o > 0)
        def _():
            piece(0, source, source).wait_recv()

        att_send[source] = attend(source)

        @pl.when(o > 0)
        def _():
            back(source, me).start()

        return 0

    lax.fori_loop(0, HEADS, step, 0)
    att_recv[me] = att_send[me]

    def finish(o, _):
        peer = lax.rem(me + o, HEADS)
        for t in range(3):
            piece(t, peer, me).wait_send()
        back(peer, me).wait_send()
        back(peer, peer).wait_recv()
        return 0

    lax.fori_loop(1, HEADS, finish, 0)
    for part in range(2):
        ow_copy(part).wait()
    joined = jnp.concatenate([att_recv[h] for h in range(HEADS)], axis=1)
    for p in range(d // 512):
        update_ref[:, p * 512 : (p + 1) * 512] = jnp.dot(
            joined, owbuf[:, :, :, p * 512 : (p + 1) * 512].reshape(inner, 512), preferred_element_type=jnp.float32
        ).astype(jnp.bfloat16)


def attention(pooled, weights):
    count, d = pooled.shape
    inner = HEADS * HEAD_DIM
    heads = (HEADS, count, HEAD_DIM)
    return pl.pallas_call(
        attend_kernel,
        out_shape=jax.ShapeDtypeStruct((count, d), jnp.bfloat16),
        in_specs=[
            pl.BlockSpec(memory_space=pltpu.VMEM),
            pl.BlockSpec(memory_space=pl.ANY),
        ],
        out_specs=pl.BlockSpec(memory_space=pltpu.VMEM),
        scratch_shapes=[
            pltpu.VMEM((count, d), jnp.bfloat16),
            pltpu.VMEM((3, HEADS, d // HEADS, inner), jnp.bfloat16),
            pltpu.VMEM((HEADS, 2, HEAD_DIM // 2, d), jnp.bfloat16),
            pltpu.VMEM((3,) + heads, jnp.bfloat16),
            pltpu.VMEM((3,) + heads, jnp.bfloat16),
            pltpu.VMEM(heads, jnp.bfloat16),
            pltpu.VMEM(heads, jnp.bfloat16),
            pltpu.SemaphoreType.DMA((3, HEADS)),
            pltpu.SemaphoreType.DMA((3, HEADS)),
            pltpu.SemaphoreType.DMA((HEADS,)),
            pltpu.SemaphoreType.DMA((HEADS,)),
            pltpu.SemaphoreType.DMA((5,)),
        ],
        compiler_params=pltpu.CompilerParams(
            collective_id=1, has_side_effects=True, vmem_limit_bytes=44 * MB),
        cost_estimate=pl.CostEstimate(
            flops=2 * count * d * 4 * inner + 4 * count * HEADS * count * inner,
            bytes_accessed=8 * d * inner, transcendentals=count * count * HEADS * HEADS),
        name="attend",
    )(pooled, weights)


def normalize(values):
    return values * lax.rsqrt(jnp.mean(values * values, axis=-1, keepdims=True) + 1e-06)


def single_head(triple):
    query_rows, key_rows, value_rows = triple
    scores = jnp.dot(query_rows, key_rows.T, preferred_element_type=jnp.float32) * HEAD_DIM ** (
        -0.5
    )
    peak = jnp.max(scores, axis=-1, keepdims=True)
    expo = jnp.exp(scores - peak)
    total = jnp.sum(expo, axis=-1, keepdims=True)
    return (
        jnp.dot(expo.astype(jnp.bfloat16), value_rows, preferred_element_type=jnp.float32) / total
    ).astype(jnp.bfloat16)


def attention_groups(pooled, qkv_weight, out_weight):
    inner = HEADS * HEAD_DIM
    count = pooled.shape[0]
    normed = normalize(pooled.astype(jnp.float32)).astype(jnp.bfloat16)
    projected = jnp.dot(
        normed,
        lax.all_gather(qkv_weight, "seq", axis=0, tiled=True),
        preferred_element_type=jnp.float32,
    ).astype(jnp.bfloat16)
    seq_count = lax.axis_size("seq")
    groups = seq_count // HEADS
    share = count // groups
    query_send = (
        projected[:, :inner]
        .reshape(groups, share, HEADS, HEAD_DIM)
        .transpose(2, 0, 1, 3)
        .reshape(seq_count, share, HEAD_DIM)
    )
    pair_send = (
        projected[:, inner:]
        .reshape(count, 2, HEADS, HEAD_DIM)
        .transpose(2, 0, 1, 3)
        .reshape(HEADS, count, 2 * HEAD_DIM)
    )
    pair_send = jnp.repeat(pair_send, groups, axis=0)
    query_recv, pair_recv = (
        lax.all_to_all(query_send, "seq", split_axis=0, concat_axis=0, tiled=True),
        lax.all_to_all(pair_send, "seq", split_axis=0, concat_axis=0, tiled=True),
    )
    key_rows = pair_recv[:, :, :HEAD_DIM].reshape(seq_count * count, HEAD_DIM)
    value_rows = pair_recv[:, :, HEAD_DIM:].reshape(seq_count * count, HEAD_DIM)

    def per_source(query_rows):
        return single_head((query_rows, key_rows, value_rows))

    head_rows = lax.map(per_source, query_recv)
    returned = lax.all_to_all(head_rows, "seq", split_axis=0, concat_axis=0, tiled=True)
    attended = (
        returned.reshape(HEADS, groups, share, HEAD_DIM).transpose(1, 2, 0, 3).reshape(count, inner)
    )
    columns = attended
    update = jnp.dot(
        columns,
        lax.all_gather(out_weight, "seq", axis=0, tiled=True),
        preferred_element_type=jnp.float32,
    )
    return update.astype(jnp.bfloat16)


def on_device(sequence, conv_weight, qkv_weight, out_weight):
    count = lax.axis_size("seq")
    if count == HEADS and lax.axis_size("dp") == DP:
        part = out_weight.shape[0] // 2
        shard = jnp.concatenate(
            [qkv_weight, jnp.concatenate([out_weight[:part], out_weight[part:]], axis=1)], axis=0)
        pooled, weights = conv_pool(sequence, conv_weight, count, shard)
        update = attention(pooled, weights)
    else:
        pooled = conv_pool(sequence, conv_weight, count)
        update = attention_groups(pooled, qkv_weight, out_weight)
    return (pooled, update)


def solution(mesh):
    return jax.shard_map(
        on_device,
        mesh=mesh,
        in_specs=(P(("dp", "seq"), None), P(), P("seq", None), P("seq", None)),
        out_specs=(P(("dp", "seq"), None), P(("dp", "seq"), None)),
        check_vma=False,
    )
```

```python
import functools

import jax
import jax.numpy as jnp
from jax import lax
from jax.experimental import pallas as pl
from jax.experimental.pallas import tpu as pltpu
from jax.sharding import PartitionSpec as P

HEADS = 8
HEAD_DIM = 128
WIDTH = 5
MESH = pl.DeviceIdType.MESH
HALO = 16
MB = 1024 * 1024
DP = 4
PAIRS = 4
REMOTE = 6
WINDOW = 2


class Gather:
    def __init__(self, shard, whole, sems):
        self.shard, self.whole = shard, whole
        self.s1, self.r1, self.s2, self.r2, self.s3, self.r3, self.own_sem = sems
        self.me = lax.axis_index("seq")
        self.dp = lax.axis_index("dp")
        self.pair, self.core = self.me // 2, self.me % 2
        self.mate = self.pair * 2 + 1 - self.core
        self.width = whole.shape[2] // (2 * DP)

    def part(self, source, group, core):
        first = pl.multiple_of((2 * group + core) * self.width, 128)
        return self.whole.at[source, :, pl.ds(first, self.width)]

    def own(self):
        return pltpu.make_async_copy(self.shard, self.whole.at[self.me], self.own_sem.at[0])

    def to_mate(self):
        return pltpu.make_async_remote_copy(
            src_ref=self.shard, dst_ref=self.whole.at[self.me], send_sem=self.s1.at[self.mate],
            recv_sem=self.r1.at[self.me], device_id={"seq": self.mate}, device_id_type=MESH)

    def from_mate(self):
        return pltpu.make_async_remote_copy(
            src_ref=self.shard, dst_ref=self.whole.at[self.mate], send_sem=self.s1.at[self.me],
            recv_sem=self.r1.at[self.mate], device_id={"seq": self.mate}, device_id_type=MESH)

    def target(self, i):
        return ((self.pair + PAIRS - 1 - i // 2) % PAIRS) * 2 + i % 2

    def source(self, i):
        return ((self.pair + 1 + i // 2) % PAIRS) * 2 + i % 2

    def out1(self, i):
        peer = self.target(i)
        first = pl.multiple_of((2 * self.dp + peer % 2) * self.width, 128)
        return pltpu.make_async_remote_copy(
            src_ref=self.shard.at[:, pl.ds(first, self.width)], dst_ref=self.part(self.me, self.dp, peer % 2),
            send_sem=self.s1.at[peer], recv_sem=self.r1.at[self.me], device_id={"seq": peer}, device_id_type=MESH)

    def in1(self, i):
        source = self.source(i)
        block = self.part(source, self.dp, self.core)
        return pltpu.make_async_remote_copy(
            src_ref=block, dst_ref=block, send_sem=self.s1.at[source], recv_sem=self.r1.at[source],
            device_id={"seq": source}, device_id_type=MESH)

    def out2(self, i, j):
        source, peer = self.source(i), (self.dp + j) % DP
        block = self.part(source, self.dp, self.core)
        return pltpu.make_async_remote_copy(
            src_ref=block, dst_ref=block, send_sem=self.s2.at[source, peer], recv_sem=self.r2.at[source, self.dp],
            device_id={"dp": peer}, device_id_type=MESH)

    def in2(self, i, j):
        source, peer = self.source(i), (self.dp + j) % DP
        block = self.part(source, peer, self.core)
        return pltpu.make_async_remote_copy(
            src_ref=block, dst_ref=block, send_sem=self.s2.at[source, peer], recv_sem=self.r2.at[source, peer],
            device_id={"dp": peer}, device_id_type=MESH)

    def out3(self, i, group):
        source = self.source(i)
        block = self.part(source, group, self.core)
        return pltpu.make_async_remote_copy(
            src_ref=block, dst_ref=block, send_sem=self.s3.at[source, group], recv_sem=self.r3.at[source, group],
            device_id={"seq": self.mate}, device_id_type=MESH)

    def in3(self, i, group):
        source = self.source(i)
        block = self.part(source, group, 1 - self.core)
        return pltpu.make_async_remote_copy(
            src_ref=block, dst_ref=block, send_sem=self.s3.at[source, group], recv_sem=self.r3.at[source, group],
            device_id={"seq": self.mate}, device_id_type=MESH)

    def start(self):
        self.own().start()
        self.to_mate().start()

        def one(i, _):
            self.out1(i).start()
            return 0

        lax.fori_loop(0, WINDOW, one, 0)

    def relay(self, i):
        self.out1(i).wait_send()

        @pl.when(i + WINDOW < REMOTE)
        def _():
            self.out1(i + WINDOW).start()

        self.in1(i).wait_recv()
        for j in range(1, DP):
            self.out2(i, j).start()
        self.out3(i, self.dp).start()

    def finish(self):
        def second(i, _):
            for j in range(1, DP):
                self.in2(i, j).wait_recv()
                self.out3(i, (self.dp + j) % DP).start()
            return 0

        lax.fori_loop(0, REMOTE, second, 0)

        def last(i, _):
            for j in range(1, DP):
                self.out2(i, j).wait_send()
            for group in range(DP):
                self.out3(i, group).wait_send()
                self.in3(i, group).wait_recv()
            return 0

        lax.fori_loop(0, REMOTE, last, 0)
        self.own().wait()
        self.to_mate().wait_send()
        self.from_mate().wait_recv()


def conv_kernel(count, share, *refs):
    if share:
        seq_ref, w_ref, shard, pooled_ref, whole, *refs = refs
    else:
        seq_ref, w_ref, pooled_ref, *refs = refs
    low, high, wbuf, ebuf, obuf, taps, send_sem, recv_sem, w_sem, *sems = refs
    gather = Gather(shard, whole, sems) if share else None
    me = lax.axis_index("seq")
    half, wide = seq_ref.shape
    d = wide // 2
    step = wbuf.shape[2]
    chunks = d // step
    has_low = me > 0
    has_high = me < count - 1
    low_id = {"seq": lax.rem(me + count - 1, count)}
    high_id = {"seq": lax.rem(me + 1, count)}

    def w_copy(c):
        return pltpu.make_async_copy(w_ref.at[:, pl.ds(c * step, step)], wbuf.at[c], w_sem.at[c])

    for c in range(chunks):
        w_copy(c).start()

    barrier = pltpu.get_barrier_semaphore()

    if share:
        for o in range(1, count):
            pl.semaphore_signal(
                barrier, inc=1, device_id={"seq": lax.rem(me + o, count)}, device_id_type=MESH)
        for o in range(1, DP):
            pl.semaphore_signal(
                barrier, inc=1, device_id={"dp": (gather.dp + o) % DP}, device_id_type=MESH)
        pl.semaphore_wait(barrier, count + DP - 2)
    else:
        for peer in (low_id, high_id):
            pl.semaphore_signal(barrier, inc=1, device_id=peer, device_id_type=MESH)
        pl.semaphore_wait(barrier, 2)

    up = pltpu.make_async_remote_copy(
        src_ref=seq_ref.at[pl.ds(half - HALO, HALO)], dst_ref=low,
        send_sem=send_sem.at[0], recv_sem=recv_sem.at[0], device_id=high_id, device_id_type=MESH)
    down = pltpu.make_async_remote_copy(
        src_ref=seq_ref.at[pl.ds(0, HALO)], dst_ref=high,
        send_sem=send_sem.at[1], recv_sem=recv_sem.at[1], device_id=low_id, device_id_type=MESH)

    @pl.when(has_high)
    def _():
        up.start()

    @pl.when(has_low)
    def _():
        down.start()

    if share:
        gather.start()

    def activate(rows):
        rows = rows.astype(jnp.float32)
        scale = lax.rsqrt(jnp.mean(rows * rows, axis=-1, keepdims=True) + 1e-06)
        return jax.nn.gelu(rows * scale)

    block = 32

    def act_step(i, _):
        r = pl.multiple_of(i * block, block)
        ebuf[pl.ds(r + 8, block), :] = activate(seq_ref[pl.ds(r, block), :d])
        obuf[pl.ds(r + 8, block), :] = activate(seq_ref[pl.ds(r, block), d:])
        return 0

    lax.fori_loop(0, half // block, act_step, 0)

    @pl.when(has_low)
    def _():
        down.wait_send()
        up.wait_recv()
        ebuf[0:8, :] = activate(low[:, :d])[8:16]
        obuf[0:8, :] = activate(low[:, d:])[8:16]

    @pl.when(jnp.logical_not(has_low))
    def _():
        ebuf[0:8, :] = jnp.zeros((8, d), jnp.float32)
        obuf[0:8, :] = jnp.zeros((8, d), jnp.float32)

    @pl.when(has_high)
    def _():
        up.wait_send()
        down.wait_recv()
        ebuf[half + 8 : half + 16, :] = activate(high[:, :d])[0:8]
        obuf[half + 8 : half + 16, :] = activate(high[:, d:])[0:8]

    @pl.when(jnp.logical_not(has_high))
    def _():
        ebuf[half + 8 : half + 16, :] = jnp.zeros((8, d), jnp.float32)
        obuf[half + 8 : half + 16, :] = jnp.zeros((8, d), jnp.float32)

    def place(c, _):
        k = pl.multiple_of(c * step, step)
        cols = pl.ds(k, step)

        def put(first, tap, value):
            taps[first : first + half, pl.ds(tap * d + k, step)] = value

        e_prev = ebuf[7 : 7 + half, cols].astype(jnp.bfloat16)
        e_here = ebuf[8 : 8 + half, cols].astype(jnp.bfloat16)
        e_next = ebuf[9 : 9 + half, cols].astype(jnp.bfloat16)
        put(0, 0, e_prev)
        put(0, 2, e_here)
        put(half, 1, e_here)
        put(0, 4, e_next)
        put(half, 3, e_next)
        o_prev = obuf[7 : 7 + half, cols].astype(jnp.bfloat16)
        o_here = obuf[8 : 8 + half, cols].astype(jnp.bfloat16)
        o_next = obuf[9 : 9 + half, cols].astype(jnp.bfloat16)
        put(0, 1, o_prev)
        put(half, 0, o_prev)
        put(0, 3, o_here)
        put(half, 2, o_here)
        put(half, 4, o_next)
        return 0

    lax.fori_loop(0, chunks, place, 0)

    def conv_step(c, _):
        if share:
            gather.relay(c)
        w_copy(c).wait()
        k = pl.multiple_of(c * step, step)
        mixed = jnp.dot(taps[...], wbuf[c], preferred_element_type=jnp.float32)
        even = mixed[:half] + seq_ref[:, pl.ds(k, step)].astype(jnp.float32)
        odd = mixed[half:] + seq_ref[:, pl.ds(k + d, step)].astype(jnp.float32)
        pooled_ref[:, pl.ds(k, step)] = jnp.maximum(even, odd).astype(jnp.bfloat16)
        return 0

    lax.fori_loop(0, chunks, conv_step, 0)
    if share:
        gather.finish()


def conv_pool(sequence, conv_weight, count, shard=None):
    rows, d = sequence.shape
    half = rows // 2
    step = 256
    pairs = sequence.reshape(half, 2 * d)
    weight = conv_weight.reshape(WIDTH * d, d)
    share = shard is not None
    out_shape = jax.ShapeDtypeStruct((half, d), jnp.bfloat16)
    out_specs = pl.BlockSpec(memory_space=pltpu.VMEM)
    in_specs = [pl.BlockSpec(memory_space=pltpu.VMEM), pl.BlockSpec(memory_space=pl.ANY)]
    operands, sems = [pairs, weight], []
    if share:
        out_shape = (out_shape, jax.ShapeDtypeStruct((count,) + shard.shape, jnp.bfloat16))
        out_specs = (out_specs, pl.BlockSpec(memory_space=pl.ANY))
        in_specs.append(pl.BlockSpec(memory_space=pl.ANY))
        operands.append(shard)
        sems = [pltpu.SemaphoreType.DMA((count,))] * 2 + [pltpu.SemaphoreType.DMA((count, DP))] * 4
        sems.append(pltpu.SemaphoreType.DMA((1,)))
    return pl.pallas_call(
        functools.partial(conv_kernel, count, share),
        out_shape=out_shape,
        in_specs=in_specs,
        out_specs=out_specs,
        scratch_shapes=[
            pltpu.VMEM((HALO, 2 * d), jnp.bfloat16),
            pltpu.VMEM((HALO, 2 * d), jnp.bfloat16),
            pltpu.VMEM((d // step, WIDTH * d, step), jnp.bfloat16),
            pltpu.VMEM((half + 16, d), jnp.float32),
            pltpu.VMEM((half + 16, d), jnp.float32),
            pltpu.VMEM((rows, WIDTH * d), jnp.bfloat16),
            pltpu.SemaphoreType.DMA((2,)),
            pltpu.SemaphoreType.DMA((2,)),
            pltpu.SemaphoreType.DMA((d // step,)),
        ] + sems,
        compiler_params=pltpu.CompilerParams(
            collective_id=0, has_side_effects=True, vmem_limit_bytes=52 * MB),
        cost_estimate=pl.CostEstimate(
            flops=2 * rows * WIDTH * d * d, bytes_accessed=2 * WIDTH * d * d, transcendentals=rows * d),
        name="conv_pool",
    )(*operands)


def attend_kernel(pooled_ref, w_ref, update_ref, normed, wbuf, owbuf, send, recv, att_send, att_recv,
                  send_sem, recv_sem, asend_sem, arecv_sem, w_sem):
    me = lax.axis_index("seq")
    count, d = pooled_ref.shape
    inner = HEADS * HEAD_DIM
    depth = d // HEADS

    def w_copy(t):
        return pltpu.make_async_copy(
            w_ref.at[:, pl.ds(0, depth), pl.ds(t * inner, inner)], wbuf.at[t], w_sem.at[t])

    def ow_copy(part):
        return pltpu.make_async_copy(
            w_ref.at[:, pl.ds(depth, HEAD_DIM // 2), pl.ds(part * d, d)], owbuf.at[:, part], w_sem.at[3 + part])

    order = (1, 2, 0)
    for t in order:
        w_copy(t).start()
    for part in range(2):
        ow_copy(part).start()

    barrier = pltpu.get_barrier_semaphore()

    def greet(o, _):
        pl.semaphore_signal(
            barrier, inc=1, device_id={"seq": lax.rem(me + o, HEADS)}, device_id_type=MESH)
        return 0

    lax.fori_loop(1, HEADS, greet, 0)

    def norm_step(i, _):
        r = pl.multiple_of(i * 32, 32)
        rows = pooled_ref[pl.ds(r, 32), :].astype(jnp.float32)
        scale = lax.rsqrt(jnp.mean(rows * rows, axis=-1, keepdims=True) + 1e-06)
        normed[pl.ds(r, 32), :] = (rows * scale).astype(jnp.bfloat16)
        return 0

    lax.fori_loop(0, count // 32, norm_step, 0)
    pl.semaphore_wait(barrier, HEADS - 1)

    def piece(t, peer, slot):
        return pltpu.make_async_remote_copy(
            src_ref=send.at[t, peer], dst_ref=recv.at[t, slot],
            send_sem=send_sem.at[t, peer], recv_sem=recv_sem.at[t, slot],
            device_id={"seq": peer}, device_id_type=MESH)

    def back(peer, slot):
        return pltpu.make_async_remote_copy(
            src_ref=att_send.at[peer], dst_ref=att_recv.at[slot],
            send_sem=asend_sem.at[peer], recv_sem=arecv_sem.at[slot],
            device_id={"seq": peer}, device_id_type=MESH)

    for t in order:
        w_copy(t).wait()

        def project(p, _, t=t):
            k = pl.multiple_of(p * 256, 256)
            both = jnp.dot(
                normed[...], wbuf[t, :, :, pl.ds(k, 256)].reshape(d, 256), preferred_element_type=jnp.float32
            ).astype(jnp.bfloat16)
            send[t, 2 * p] = both[:, :HEAD_DIM]
            send[t, 2 * p + 1] = both[:, HEAD_DIM:]
            return 0

        lax.fori_loop(0, HEADS // 2, project, 0)

        def post(o, _, t=t):
            piece(t, lax.rem(me + o, HEADS), me).start()
            return 0

        lax.fori_loop(1, HEADS, post, 0)
        recv[t, me] = send[t, me]

    def arrive(t):
        def one(o, _):
            source = lax.rem(me + HEADS - o, HEADS)
            piece(t, source, source).wait_recv()
            return 0

        lax.fori_loop(1, HEADS, one, 0)

    arrive(1)
    arrive(2)
    keys = recv.at[1]
    values = recv.at[2]
    factor = HEAD_DIM ** (-0.5) * 1.4426950408889634

    def attend(source):
        total_rows = HEADS * count
        raw = lax.dot_general(
            recv[0, source], keys[...].reshape(total_rows, HEAD_DIM),
            (((1,), (1,)), ((), ())), preferred_element_type=jnp.float32)
        peak = jnp.max(raw, axis=-1, keepdims=True)
        expo = jnp.exp2((raw - peak) * factor)
        total = jnp.sum(expo, axis=-1, keepdims=True)
        weighted = jnp.dot(
            expo.astype(jnp.bfloat16), values[...].reshape(total_rows, HEAD_DIM),
            preferred_element_type=jnp.float32)
        return (weighted / total).astype(jnp.bfloat16)

    def step(o, _):
        source = lax.rem(me + HEADS - o, HEADS)

        @pl.when(o > 0)
        def _():
            piece(0, source, source).wait_recv()

        att_send[source] = attend(source)

        @pl.when(o > 0)
        def _():
            back(source, me).start()

        return 0

    lax.fori_loop(0, HEADS, step, 0)
    att_recv[me] = att_send[me]

    def finish(o, _):
        peer = lax.rem(me + o, HEADS)
        for t in range(3):
            piece(t, peer, me).wait_send()
        back(peer, me).wait_send()
        back(peer, peer).wait_recv()
        return 0

    lax.fori_loop(1, HEADS, finish, 0)
    for part in range(2):
        ow_copy(part).wait()
    joined = jnp.concatenate([att_recv[h] for h in range(HEADS)], axis=1)
    for p in range(d // 512):
        update_ref[:, p * 512 : (p + 1) * 512] = jnp.dot(
            joined, owbuf[:, :, :, p * 512 : (p + 1) * 512].reshape(inner, 512), preferred_element_type=jnp.float32
        ).astype(jnp.bfloat16)


def attention(pooled, weights):
    count, d = pooled.shape
    inner = HEADS * HEAD_DIM
    heads = (HEADS, count, HEAD_DIM)
    return pl.pallas_call(
        attend_kernel,
        out_shape=jax.ShapeDtypeStruct((count, d), jnp.bfloat16),
        in_specs=[
            pl.BlockSpec(memory_space=pltpu.VMEM),
            pl.BlockSpec(memory_space=pl.ANY),
        ],
        out_specs=pl.BlockSpec(memory_space=pltpu.VMEM),
        scratch_shapes=[
            pltpu.VMEM((count, d), jnp.bfloat16),
            pltpu.VMEM((3, HEADS, d // HEADS, inner), jnp.bfloat16),
            pltpu.VMEM((HEADS, 2, HEAD_DIM // 2, d), jnp.bfloat16),
            pltpu.VMEM((3,) + heads, jnp.bfloat16),
            pltpu.VMEM((3,) + heads, jnp.bfloat16),
            pltpu.VMEM(heads, jnp.bfloat16),
            pltpu.VMEM(heads, jnp.bfloat16),
            pltpu.SemaphoreType.DMA((3, HEADS)),
            pltpu.SemaphoreType.DMA((3, HEADS)),
            pltpu.SemaphoreType.DMA((HEADS,)),
            pltpu.SemaphoreType.DMA((HEADS,)),
            pltpu.SemaphoreType.DMA((5,)),
        ],
        compiler_params=pltpu.CompilerParams(
            collective_id=1, has_side_effects=True, vmem_limit_bytes=44 * MB),
        cost_estimate=pl.CostEstimate(
            flops=2 * count * d * 4 * inner + 4 * count * HEADS * count * inner,
            bytes_accessed=8 * d * inner, transcendentals=count * count * HEADS * HEADS),
        name="attend",
    )(pooled, weights)


def normalize(values):
    return values * lax.rsqrt(jnp.mean(values * values, axis=-1, keepdims=True) + 1e-06)


def single_head(triple):
    query_rows, key_rows, value_rows = triple
    scores = jnp.dot(query_rows, key_rows.T, preferred_element_type=jnp.float32) * HEAD_DIM ** (
        -0.5
    )
    peak = jnp.max(scores, axis=-1, keepdims=True)
    expo = jnp.exp(scores - peak)
    total = jnp.sum(expo, axis=-1, keepdims=True)
    return (
        jnp.dot(expo.astype(jnp.bfloat16), value_rows, preferred_element_type=jnp.float32) / total
    ).astype(jnp.bfloat16)


def attention_groups(pooled, qkv_weight, out_weight):
    inner = HEADS * HEAD_DIM
    count = pooled.shape[0]
    normed = normalize(pooled.astype(jnp.float32)).astype(jnp.bfloat16)
    projected = jnp.dot(
        normed,
        lax.all_gather(qkv_weight, "seq", axis=0, tiled=True),
        preferred_element_type=jnp.float32,
    ).astype(jnp.bfloat16)
    seq_count = lax.axis_size("seq")
    groups = seq_count // HEADS
    share = count // groups
    query_send = (
        projected[:, :inner]
        .reshape(groups, share, HEADS, HEAD_DIM)
        .transpose(2, 0, 1, 3)
        .reshape(seq_count, share, HEAD_DIM)
    )
    pair_send = (
        projected[:, inner:]
        .reshape(count, 2, HEADS, HEAD_DIM)
        .transpose(2, 0, 1, 3)
        .reshape(HEADS, count, 2 * HEAD_DIM)
    )
    pair_send = jnp.repeat(pair_send, groups, axis=0)
    query_recv, pair_recv = (
        lax.all_to_all(query_send, "seq", split_axis=0, concat_axis=0, tiled=True),
        lax.all_to_all(pair_send, "seq", split_axis=0, concat_axis=0, tiled=True),
    )
    key_rows = pair_recv[:, :, :HEAD_DIM].reshape(seq_count * count, HEAD_DIM)
    value_rows = pair_recv[:, :, HEAD_DIM:].reshape(seq_count * count, HEAD_DIM)

    def per_source(query_rows):
        return single_head((query_rows, key_rows, value_rows))

    head_rows = lax.map(per_source, query_recv)
    returned = lax.all_to_all(head_rows, "seq", split_axis=0, concat_axis=0, tiled=True)
    attended = (
        returned.reshape(HEADS, groups, share, HEAD_DIM).transpose(1, 2, 0, 3).reshape(count, inner)
    )
    columns = attended
    update = jnp.dot(
        columns,
        lax.all_gather(out_weight, "seq", axis=0, tiled=True),
        preferred_element_type=jnp.float32,
    )
    return update.astype(jnp.bfloat16)


def on_device(sequence, conv_weight, qkv_weight, out_weight):
    count = lax.axis_size("seq")
    if count == HEADS and lax.axis_size("dp") == DP:
        part = out_weight.shape[0] // 2
        shard = jnp.concatenate(
            [qkv_weight, jnp.concatenate([out_weight[:part], out_weight[part:]], axis=1)], axis=0)
        pooled, weights = conv_pool(sequence, conv_weight, count, shard)
        update = attention(pooled, weights)
    else:
        pooled = conv_pool(sequence, conv_weight, count)
        update = attention_groups(pooled, qkv_weight, out_weight)
    return (pooled, update)


def solution(mesh):
    return jax.shard_map(
        on_device,
        mesh=mesh,
        in_specs=(P(("dp", "seq"), None), P(), P("seq", None), P("seq", None)),
        out_specs=(P(("dp", "seq"), None), P(("dp", "seq"), None)),
        check_vma=False,
    )
```

```python
import functools

import jax
import jax.numpy as jnp
from jax import lax
from jax.experimental import pallas as pl
from jax.experimental.pallas import tpu as pltpu
from jax.sharding import PartitionSpec as P

HEADS = 8
HEAD_DIM = 128
WIDTH = 5
MESH = pl.DeviceIdType.MESH
HALO = 16
MB = 1024 * 1024
DP = 4
PAIRS = 4
REMOTE = 6
WINDOW = 2


class Gather:
    def __init__(self, shard, whole, sems):
        self.shard, self.whole = shard, whole
        self.s1, self.r1, self.s2, self.r2, self.s3, self.r3, self.own_sem = sems
        self.me = lax.axis_index("seq")
        self.dp = lax.axis_index("dp")
        self.pair, self.core = self.me // 2, self.me % 2
        self.mate = self.pair * 2 + 1 - self.core
        self.width = whole.shape[2] // (2 * DP)

    def part(self, source, group, core):
        first = pl.multiple_of((2 * group + core) * self.width, 128)
        return self.whole.at[source, :, pl.ds(first, self.width)]

    def own(self):
        return pltpu.make_async_copy(self.shard, self.whole.at[self.me], self.own_sem.at[0])

    def to_mate(self):
        return pltpu.make_async_remote_copy(
            src_ref=self.shard, dst_ref=self.whole.at[self.me], send_sem=self.s1.at[self.mate],
            recv_sem=self.r1.at[self.me], device_id={"seq": self.mate}, device_id_type=MESH)

    def from_mate(self):
        return pltpu.make_async_remote_copy(
            src_ref=self.shard, dst_ref=self.whole.at[self.mate], send_sem=self.s1.at[self.me],
            recv_sem=self.r1.at[self.mate], device_id={"seq": self.mate}, device_id_type=MESH)

    def target(self, i):
        return ((self.pair + PAIRS - 1 - i // 2) % PAIRS) * 2 + i % 2

    def source(self, i):
        return ((self.pair + 1 + i // 2) % PAIRS) * 2 + i % 2

    def out1(self, i):
        peer = self.target(i)
        first = pl.multiple_of((2 * self.dp + peer % 2) * self.width, 128)
        return pltpu.make_async_remote_copy(
            src_ref=self.shard.at[:, pl.ds(first, self.width)], dst_ref=self.part(self.me, self.dp, peer % 2),
            send_sem=self.s1.at[peer], recv_sem=self.r1.at[self.me], device_id={"seq": peer}, device_id_type=MESH)

    def in1(self, i):
        source = self.source(i)
        block = self.part(source, self.dp, self.core)
        return pltpu.make_async_remote_copy(
            src_ref=block, dst_ref=block, send_sem=self.s1.at[source], recv_sem=self.r1.at[source],
            device_id={"seq": source}, device_id_type=MESH)

    def out2(self, i, j):
        source, peer = self.source(i), (self.dp + j) % DP
        block = self.part(source, self.dp, self.core)
        return pltpu.make_async_remote_copy(
            src_ref=block, dst_ref=block, send_sem=self.s2.at[source, peer], recv_sem=self.r2.at[source, self.dp],
            device_id={"dp": peer}, device_id_type=MESH)

    def in2(self, i, j):
        source, peer = self.source(i), (self.dp + j) % DP
        block = self.part(source, peer, self.core)
        return pltpu.make_async_remote_copy(
            src_ref=block, dst_ref=block, send_sem=self.s2.at[source, peer], recv_sem=self.r2.at[source, peer],
            device_id={"dp": peer}, device_id_type=MESH)

    def out3(self, i, group):
        source = self.source(i)
        block = self.part(source, group, self.core)
        return pltpu.make_async_remote_copy(
            src_ref=block, dst_ref=block, send_sem=self.s3.at[source, group], recv_sem=self.r3.at[source, group],
            device_id={"seq": self.mate}, device_id_type=MESH)

    def in3(self, i, group):
        source = self.source(i)
        block = self.part(source, group, 1 - self.core)
        return pltpu.make_async_remote_copy(
            src_ref=block, dst_ref=block, send_sem=self.s3.at[source, group], recv_sem=self.r3.at[source, group],
            device_id={"seq": self.mate}, device_id_type=MESH)

    def start(self):
        self.own().start()
        self.to_mate().start()

        def one(i, _):
            self.out1(i).start()
            return 0

        lax.fori_loop(0, WINDOW, one, 0)

    def relay(self, i):
        self.out1(i).wait_send()

        @pl.when(i + WINDOW < REMOTE)
        def _():
            self.out1(i + WINDOW).start()

        self.in1(i).wait_recv()
        for j in range(1, DP):
            self.out2(i, j).start()
        self.out3(i, self.dp).start()

    def finish(self):
        def second(i, _):
            for j in range(1, DP):
                self.in2(i, j).wait_recv()
                self.out3(i, (self.dp + j) % DP).start()
            return 0

        lax.fori_loop(0, REMOTE, second, 0)

        def last(i, _):
            for j in range(1, DP):
                self.out2(i, j).wait_send()
            for group in range(DP):
                self.out3(i, group).wait_send()
                self.in3(i, group).wait_recv()
            return 0

        lax.fori_loop(0, REMOTE, last, 0)
        self.own().wait()
        self.to_mate().wait_send()
        self.from_mate().wait_recv()


def conv_kernel(count, share, *refs):
    if share:
        seq_ref, w_ref, shard, pooled_ref, whole, *refs = refs
    else:
        seq_ref, w_ref, pooled_ref, *refs = refs
    low, high, wbuf, ebuf, obuf, taps, send_sem, recv_sem, w_sem, *sems = refs
    gather = Gather(shard, whole, sems) if share else None
    me = lax.axis_index("seq")
    half, wide = seq_ref.shape
    d = wide // 2
    step = wbuf.shape[2]
    chunks = d // step
    has_low = me > 0
    has_high = me < count - 1
    low_id = {"seq": lax.rem(me + count - 1, count)}
    high_id = {"seq": lax.rem(me + 1, count)}

    def w_copy(c):
        return pltpu.make_async_copy(w_ref.at[:, pl.ds(c * step, step)], wbuf.at[c], w_sem.at[c])

    for c in range(chunks):
        w_copy(c).start()

    barrier = pltpu.get_barrier_semaphore()

    if share:
        for o in range(1, count):
            pl.semaphore_signal(
                barrier, inc=1, device_id={"seq": lax.rem(me + o, count)}, device_id_type=MESH)
        for o in range(1, DP):
            pl.semaphore_signal(
                barrier, inc=1, device_id={"dp": (gather.dp + o) % DP}, device_id_type=MESH)
        pl.semaphore_wait(barrier, count + DP - 2)
    else:
        for peer in (low_id, high_id):
            pl.semaphore_signal(barrier, inc=1, device_id=peer, device_id_type=MESH)
        pl.semaphore_wait(barrier, 2)

    up = pltpu.make_async_remote_copy(
        src_ref=seq_ref.at[pl.ds(half - HALO, HALO)], dst_ref=low,
        send_sem=send_sem.at[0], recv_sem=recv_sem.at[0], device_id=high_id, device_id_type=MESH)
    down = pltpu.make_async_remote_copy(
        src_ref=seq_ref.at[pl.ds(0, HALO)], dst_ref=high,
        send_sem=send_sem.at[1], recv_sem=recv_sem.at[1], device_id=low_id, device_id_type=MESH)

    @pl.when(has_high)
    def _():
        up.start()

    @pl.when(has_low)
    def _():
        down.start()

    if share:
        gather.start()

    def activate(rows):
        rows = rows.astype(jnp.float32)
        scale = lax.rsqrt(jnp.mean(rows * rows, axis=-1, keepdims=True) + 1e-06)
        return jax.nn.gelu(rows * scale)

    block = 32

    def act_step(i, _):
        r = pl.multiple_of(i * block, block)
        ebuf[pl.ds(r + 8, block), :] = activate(seq_ref[pl.ds(r, block), :d])
        obuf[pl.ds(r + 8, block), :] = activate(seq_ref[pl.ds(r, block), d:])
        return 0

    lax.fori_loop(0, half // block, act_step, 0)

    @pl.when(has_low)
    def _():
        down.wait_send()
        up.wait_recv()
        ebuf[0:8, :] = activate(low[:, :d])[8:16]
        obuf[0:8, :] = activate(low[:, d:])[8:16]

    @pl.when(jnp.logical_not(has_low))
    def _():
        ebuf[0:8, :] = jnp.zeros((8, d), jnp.float32)
        obuf[0:8, :] = jnp.zeros((8, d), jnp.float32)

    @pl.when(has_high)
    def _():
        up.wait_send()
        down.wait_recv()
        ebuf[half + 8 : half + 16, :] = activate(high[:, :d])[0:8]
        obuf[half + 8 : half + 16, :] = activate(high[:, d:])[0:8]

    @pl.when(jnp.logical_not(has_high))
    def _():
        ebuf[half + 8 : half + 16, :] = jnp.zeros((8, d), jnp.float32)
        obuf[half + 8 : half + 16, :] = jnp.zeros((8, d), jnp.float32)

    def place(c, _):
        k = pl.multiple_of(c * step, step)
        cols = pl.ds(k, step)

        def put(first, tap, value):
            taps[first : first + half, pl.ds(tap * d + k, step)] = value

        e_prev = ebuf[7 : 7 + half, cols].astype(jnp.bfloat16)
        e_here = ebuf[8 : 8 + half, cols].astype(jnp.bfloat16)
        e_next = ebuf[9 : 9 + half, cols].astype(jnp.bfloat16)
        put(0, 0, e_prev)
        put(0, 2, e_here)
        put(half, 1, e_here)
        put(0, 4, e_next)
        put(half, 3, e_next)
        o_prev = obuf[7 : 7 + half, cols].astype(jnp.bfloat16)
        o_here = obuf[8 : 8 + half, cols].astype(jnp.bfloat16)
        o_next = obuf[9 : 9 + half, cols].astype(jnp.bfloat16)
        put(0, 1, o_prev)
        put(half, 0, o_prev)
        put(0, 3, o_here)
        put(half, 2, o_here)
        put(half, 4, o_next)
        return 0

    lax.fori_loop(0, chunks, place, 0)

    def conv_step(c, _):
        if share:
            gather.relay(c)
        w_copy(c).wait()
        k = pl.multiple_of(c * step, step)
        mixed = jnp.dot(taps[...], wbuf[c], preferred_element_type=jnp.float32)
        even = mixed[:half] + seq_ref[:, pl.ds(k, step)].astype(jnp.float32)
        odd = mixed[half:] + seq_ref[:, pl.ds(k + d, step)].astype(jnp.float32)
        pooled_ref[:, pl.ds(k, step)] = jnp.maximum(even, odd).astype(jnp.bfloat16)
        return 0

    lax.fori_loop(0, chunks, conv_step, 0)
    if share:
        gather.finish()


def conv_pool(sequence, conv_weight, count, shard=None):
    rows, d = sequence.shape
    half = rows // 2
    step = 256
    pairs = sequence.reshape(half, 2 * d)
    weight = conv_weight.reshape(WIDTH * d, d)
    share = shard is not None
    out_shape = jax.ShapeDtypeStruct((half, d), jnp.bfloat16)
    out_specs = pl.BlockSpec(memory_space=pltpu.VMEM)
    in_specs = [pl.BlockSpec(memory_space=pltpu.VMEM), pl.BlockSpec(memory_space=pl.ANY)]
    operands, sems = [pairs, weight], []
    if share:
        out_shape = (out_shape, jax.ShapeDtypeStruct((count,) + shard.shape, jnp.bfloat16))
        out_specs = (out_specs, pl.BlockSpec(memory_space=pl.ANY))
        in_specs.append(pl.BlockSpec(memory_space=pl.ANY))
        operands.append(shard)
        sems = [pltpu.SemaphoreType.DMA((count,))] * 2 + [pltpu.SemaphoreType.DMA((count, DP))] * 4
        sems.append(pltpu.SemaphoreType.DMA((1,)))
    return pl.pallas_call(
        functools.partial(conv_kernel, count, share),
        out_shape=out_shape,
        in_specs=in_specs,
        out_specs=out_specs,
        scratch_shapes=[
            pltpu.VMEM((HALO, 2 * d), jnp.bfloat16),
            pltpu.VMEM((HALO, 2 * d), jnp.bfloat16),
            pltpu.VMEM((d // step, WIDTH * d, step), jnp.bfloat16),
            pltpu.VMEM((half + 16, d), jnp.float32),
            pltpu.VMEM((half + 16, d), jnp.float32),
            pltpu.VMEM((rows, WIDTH * d), jnp.bfloat16),
            pltpu.SemaphoreType.DMA((2,)),
            pltpu.SemaphoreType.DMA((2,)),
            pltpu.SemaphoreType.DMA((d // step,)),
        ] + sems,
        compiler_params=pltpu.CompilerParams(
            collective_id=0, has_side_effects=True, vmem_limit_bytes=52 * MB),
        cost_estimate=pl.CostEstimate(
            flops=2 * rows * WIDTH * d * d, bytes_accessed=2 * WIDTH * d * d, transcendentals=rows * d),
        name="conv_pool",
    )(*operands)


def attend_kernel(pooled_ref, w_ref, out_w_ref, update_ref, normed, wbuf, owbuf, send, recv, att_send, att_recv,
                  send_sem, recv_sem, asend_sem, arecv_sem, w_sem):
    me = lax.axis_index("seq")
    count, d = pooled_ref.shape
    inner = HEADS * HEAD_DIM

    def w_copy(t):
        return pltpu.make_async_copy(w_ref.at[:, :, pl.ds(t * inner, inner)], wbuf.at[t], w_sem.at[t])

    ow_copy = pltpu.make_async_copy(out_w_ref, owbuf, w_sem.at[3])
    order = (1, 2, 0)
    for t in order:
        w_copy(t).start()
    ow_copy.start()

    barrier = pltpu.get_barrier_semaphore()

    def greet(o, _):
        pl.semaphore_signal(
            barrier, inc=1, device_id={"seq": lax.rem(me + o, HEADS)}, device_id_type=MESH)
        return 0

    lax.fori_loop(1, HEADS, greet, 0)

    def norm_step(i, _):
        r = pl.multiple_of(i * 32, 32)
        rows = pooled_ref[pl.ds(r, 32), :].astype(jnp.float32)
        scale = lax.rsqrt(jnp.mean(rows * rows, axis=-1, keepdims=True) + 1e-06)
        normed[pl.ds(r, 32), :] = (rows * scale).astype(jnp.bfloat16)
        return 0

    lax.fori_loop(0, count // 32, norm_step, 0)
    pl.semaphore_wait(barrier, HEADS - 1)

    def piece(t, peer, slot):
        return pltpu.make_async_remote_copy(
            src_ref=send.at[t, peer], dst_ref=recv.at[t, slot],
            send_sem=send_sem.at[t, peer], recv_sem=recv_sem.at[t, slot],
            device_id={"seq": peer}, device_id_type=MESH)

    def back(peer, slot):
        return pltpu.make_async_remote_copy(
            src_ref=att_send.at[peer], dst_ref=att_recv.at[slot],
            send_sem=asend_sem.at[peer], recv_sem=arecv_sem.at[slot],
            device_id={"seq": peer}, device_id_type=MESH)

    for t in order:
        w_copy(t).wait()

        def project(p, _, t=t):
            k = pl.multiple_of(p * 256, 256)
            both = jnp.dot(
                normed[...], wbuf[t, :, :, pl.ds(k, 256)].reshape(d, 256), preferred_element_type=jnp.float32
            ).astype(jnp.bfloat16)
            send[t, 2 * p] = both[:, :HEAD_DIM]
            send[t, 2 * p + 1] = both[:, HEAD_DIM:]
            return 0

        lax.fori_loop(0, HEADS // 2, project, 0)

        def post(o, _, t=t):
            piece(t, lax.rem(me + o, HEADS), me).start()
            return 0

        lax.fori_loop(1, HEADS, post, 0)
        recv[t, me] = send[t, me]

    def arrive(t):
        def one(o, _):
            source = lax.rem(me + HEADS - o, HEADS)
            piece(t, source, source).wait_recv()
            return 0

        lax.fori_loop(1, HEADS, one, 0)

    arrive(1)
    arrive(2)
    keys = recv.at[1]
    values = recv.at[2]
    factor = HEAD_DIM ** (-0.5) * 1.4426950408889634

    def attend(source):
        total_rows = HEADS * count
        raw = lax.dot_general(
            recv[0, source], keys[...].reshape(total_rows, HEAD_DIM),
            (((1,), (1,)), ((), ())), preferred_element_type=jnp.float32)
        peak = jnp.max(raw, axis=-1, keepdims=True)
        expo = jnp.exp2((raw - peak) * factor)
        total = jnp.sum(expo, axis=-1, keepdims=True)
        weighted = jnp.dot(
            expo.astype(jnp.bfloat16), values[...].reshape(total_rows, HEAD_DIM),
            preferred_element_type=jnp.float32)
        return (weighted / total).astype(jnp.bfloat16)

    def step(o, _):
        source = lax.rem(me + HEADS - o, HEADS)

        @pl.when(o > 0)
        def _():
            piece(0, source, source).wait_recv()

        att_send[source] = attend(source)

        @pl.when(o > 0)
        def _():
            back(source, me).start()

        return 0

    lax.fori_loop(0, HEADS, step, 0)
    att_recv[me] = att_send[me]

    def finish(o, _):
        peer = lax.rem(me + o, HEADS)
        for t in range(3):
            piece(t, peer, me).wait_send()
        back(peer, me).wait_send()
        back(peer, peer).wait_recv()
        return 0

    lax.fori_loop(1, HEADS, finish, 0)
    ow_copy.wait()
    joined = jnp.concatenate([att_recv[h] for h in range(HEADS)], axis=1)
    for p in range(d // 512):
        update_ref[:, p * 512 : (p + 1) * 512] = jnp.dot(
            joined, owbuf[:, p * 512 : (p + 1) * 512], preferred_element_type=jnp.float32
        ).astype(jnp.bfloat16)


def attention(pooled, weights, out_weight):
    count, d = pooled.shape
    inner = HEADS * HEAD_DIM
    heads = (HEADS, count, HEAD_DIM)
    return pl.pallas_call(
        attend_kernel,
        out_shape=jax.ShapeDtypeStruct((count, d), jnp.bfloat16),
        in_specs=[
            pl.BlockSpec(memory_space=pltpu.VMEM),
            pl.BlockSpec(memory_space=pl.ANY),
            pl.BlockSpec(memory_space=pl.ANY),
        ],
        out_specs=pl.BlockSpec(memory_space=pltpu.VMEM),
        scratch_shapes=[
            pltpu.VMEM((count, d), jnp.bfloat16),
            pltpu.VMEM((3, HEADS, d // HEADS, inner), jnp.bfloat16),
            pltpu.VMEM((inner, d), jnp.bfloat16),
            pltpu.VMEM((3,) + heads, jnp.bfloat16),
            pltpu.VMEM((3,) + heads, jnp.bfloat16),
            pltpu.VMEM(heads, jnp.bfloat16),
            pltpu.VMEM(heads, jnp.bfloat16),
            pltpu.SemaphoreType.DMA((3, HEADS)),
            pltpu.SemaphoreType.DMA((3, HEADS)),
            pltpu.SemaphoreType.DMA((HEADS,)),
            pltpu.SemaphoreType.DMA((HEADS,)),
            pltpu.SemaphoreType.DMA((4,)),
        ],
        compiler_params=pltpu.CompilerParams(
            collective_id=1, has_side_effects=True, vmem_limit_bytes=44 * MB),
        cost_estimate=pl.CostEstimate(
            flops=2 * count * d * 4 * inner + 4 * count * HEADS * count * inner,
            bytes_accessed=8 * d * inner, transcendentals=count * count * HEADS * HEADS),
        name="attend",
    )(pooled, weights, out_weight)


def normalize(values):
    return values * lax.rsqrt(jnp.mean(values * values, axis=-1, keepdims=True) + 1e-06)


def single_head(triple):
    query_rows, key_rows, value_rows = triple
    scores = jnp.dot(query_rows, key_rows.T, preferred_element_type=jnp.float32) * HEAD_DIM ** (
        -0.5
    )
    peak = jnp.max(scores, axis=-1, keepdims=True)
    expo = jnp.exp(scores - peak)
    total = jnp.sum(expo, axis=-1, keepdims=True)
    return (
        jnp.dot(expo.astype(jnp.bfloat16), value_rows, preferred_element_type=jnp.float32) / total
    ).astype(jnp.bfloat16)


def attention_groups(pooled, qkv_weight, out_weight):
    inner = HEADS * HEAD_DIM
    count = pooled.shape[0]
    normed = normalize(pooled.astype(jnp.float32)).astype(jnp.bfloat16)
    projected = jnp.dot(
        normed,
        lax.all_gather(qkv_weight, "seq", axis=0, tiled=True),
        preferred_element_type=jnp.float32,
    ).astype(jnp.bfloat16)
    seq_count = lax.axis_size("seq")
    groups = seq_count // HEADS
    share = count // groups
    query_send = (
        projected[:, :inner]
        .reshape(groups, share, HEADS, HEAD_DIM)
        .transpose(2, 0, 1, 3)
        .reshape(seq_count, share, HEAD_DIM)
    )
    pair_send = (
        projected[:, inner:]
        .reshape(count, 2, HEADS, HEAD_DIM)
        .transpose(2, 0, 1, 3)
        .reshape(HEADS, count, 2 * HEAD_DIM)
    )
    pair_send = jnp.repeat(pair_send, groups, axis=0)
    query_recv, pair_recv = (
        lax.all_to_all(query_send, "seq", split_axis=0, concat_axis=0, tiled=True),
        lax.all_to_all(pair_send, "seq", split_axis=0, concat_axis=0, tiled=True),
    )
    key_rows = pair_recv[:, :, :HEAD_DIM].reshape(seq_count * count, HEAD_DIM)
    value_rows = pair_recv[:, :, HEAD_DIM:].reshape(seq_count * count, HEAD_DIM)

    def per_source(query_rows):
        return single_head((query_rows, key_rows, value_rows))

    head_rows = lax.map(per_source, query_recv)
    returned = lax.all_to_all(head_rows, "seq", split_axis=0, concat_axis=0, tiled=True)
    attended = (
        returned.reshape(HEADS, groups, share, HEAD_DIM).transpose(1, 2, 0, 3).reshape(count, inner)
    )
    columns = attended
    update = jnp.dot(
        columns,
        lax.all_gather(out_weight, "seq", axis=0, tiled=True),
        preferred_element_type=jnp.float32,
    )
    return update.astype(jnp.bfloat16)


def on_device(sequence, conv_weight, qkv_weight, out_weight):
    count = lax.axis_size("seq")
    if count == HEADS and lax.axis_size("dp") == DP:
        outer = lax.all_gather(out_weight, "seq", axis=0, tiled=True)
        pooled, weights = conv_pool(sequence, conv_weight, count, qkv_weight)
        update = attention(pooled, weights, outer)
    else:
        pooled = conv_pool(sequence, conv_weight, count)
        update = attention_groups(pooled, qkv_weight, out_weight)
    return (pooled, update)


def solution(mesh):
    return jax.shard_map(
        on_device,
        mesh=mesh,
        in_specs=(P(("dp", "seq"), None), P(), P("seq", None), P("seq", None)),
        out_specs=(P(("dp", "seq"), None), P(("dp", "seq"), None)),
        check_vma=False,
    )
```

```python
import functools

import jax
import jax.numpy as jnp
from jax import lax
from jax.experimental import pallas as pl
from jax.experimental.pallas import tpu as pltpu
from jax.sharding import PartitionSpec as P

HEADS = 8
HEAD_DIM = 128
WIDTH = 5
MESH = pl.DeviceIdType.MESH
HALO = 16
MB = 1024 * 1024
DP = 4
PAIRS = 4
REMOTE = 6
WINDOW = 2
LAG = 2


class Gather:
    def __init__(self, shard, whole, sems):
        self.shard, self.whole = shard, whole
        self.s1, self.r1, self.s2, self.r2, self.s3, self.r3, self.own_sem = sems
        self.me = lax.axis_index("seq")
        self.dp = lax.axis_index("dp")
        self.pair, self.core = self.me // 2, self.me % 2
        self.mate = self.pair * 2 + 1 - self.core
        self.width = whole.shape[1] // (2 * DP)

    def part(self, source, group, core):
        first = pl.multiple_of((2 * group + core) * self.width, self.width)
        return self.whole.at[source, pl.ds(first, self.width)]

    def own(self):
        return pltpu.make_async_copy(self.shard, self.whole.at[self.me], self.own_sem.at[0])

    def to_mate(self):
        return pltpu.make_async_remote_copy(
            src_ref=self.shard, dst_ref=self.whole.at[self.me], send_sem=self.s1.at[self.mate],
            recv_sem=self.r1.at[self.me], device_id={"seq": self.mate}, device_id_type=MESH)

    def from_mate(self):
        return pltpu.make_async_remote_copy(
            src_ref=self.shard, dst_ref=self.whole.at[self.mate], send_sem=self.s1.at[self.me],
            recv_sem=self.r1.at[self.mate], device_id={"seq": self.mate}, device_id_type=MESH)

    def target(self, i):
        return ((self.pair + PAIRS - 1 - i // 2) % PAIRS) * 2 + i % 2

    def source(self, i):
        return ((self.pair + 1 + i // 2) % PAIRS) * 2 + i % 2

    def out1(self, i):
        peer = self.target(i)
        first = pl.multiple_of((2 * self.dp + peer % 2) * self.width, self.width)
        return pltpu.make_async_remote_copy(
            src_ref=self.shard.at[pl.ds(first, self.width)], dst_ref=self.part(self.me, self.dp, peer % 2),
            send_sem=self.s1.at[peer], recv_sem=self.r1.at[self.me], device_id={"seq": peer}, device_id_type=MESH)

    def in1(self, i):
        source = self.source(i)
        block = self.part(source, self.dp, self.core)
        return pltpu.make_async_remote_copy(
            src_ref=block, dst_ref=block, send_sem=self.s1.at[source], recv_sem=self.r1.at[source],
            device_id={"seq": source}, device_id_type=MESH)

    def out2(self, i, j):
        source, peer = self.source(i), (self.dp + j) % DP
        block = self.part(source, self.dp, self.core)
        return pltpu.make_async_remote_copy(
            src_ref=block, dst_ref=block, send_sem=self.s2.at[source, peer], recv_sem=self.r2.at[source, self.dp],
            device_id={"dp": peer}, device_id_type=MESH)

    def in2(self, i, j):
        source, peer = self.source(i), (self.dp + j) % DP
        block = self.part(source, peer, self.core)
        return pltpu.make_async_remote_copy(
            src_ref=block, dst_ref=block, send_sem=self.s2.at[source, peer], recv_sem=self.r2.at[source, peer],
            device_id={"dp": peer}, device_id_type=MESH)

    def out3(self, i, group):
        source = self.source(i)
        block = self.part(source, group, self.core)
        return pltpu.make_async_remote_copy(
            src_ref=block, dst_ref=block, send_sem=self.s3.at[source, group], recv_sem=self.r3.at[source, group],
            device_id={"seq": self.mate}, device_id_type=MESH)

    def in3(self, i, group):
        source = self.source(i)
        block = self.part(source, group, 1 - self.core)
        return pltpu.make_async_remote_copy(
            src_ref=block, dst_ref=block, send_sem=self.s3.at[source, group], recv_sem=self.r3.at[source, group],
            device_id={"seq": self.mate}, device_id_type=MESH)

    def start(self):
        self.own().start()
        self.to_mate().start()

        def one(i, _):
            self.out1(i).start()
            return 0

        lax.fori_loop(0, WINDOW, one, 0)

    def relay(self, i):
        self.out1(i).wait_send()

        @pl.when(i + WINDOW < REMOTE)
        def _():
            self.out1(i + WINDOW).start()

        self.in1(i).wait_recv()
        for j in range(1, DP):
            self.out2(i, j).start()
        self.out3(i, self.dp).start()

    def second(self, i):
        for j in range(1, DP):
            self.in2(i, j).wait_recv()
            self.out3(i, (self.dp + j) % DP).start()

    def finish(self):
        def rest(i, _):
            self.second(i)
            return 0

        lax.fori_loop(REMOTE - LAG, REMOTE, rest, 0)

        def last(i, _):
            for j in range(1, DP):
                self.out2(i, j).wait_send()
            for group in range(DP):
                self.out3(i, group).wait_send()
                self.in3(i, group).wait_recv()
            return 0

        lax.fori_loop(0, REMOTE, last, 0)
        self.own().wait()
        self.to_mate().wait_send()
        self.from_mate().wait_recv()


def conv_kernel(count, share, *refs):
    if share:
        seq_ref, w_ref, shard, pooled_ref, whole, *refs = refs
    else:
        seq_ref, w_ref, pooled_ref, *refs = refs
    low, high, wbuf, ebuf, obuf, taps, send_sem, recv_sem, w_sem, *sems = refs
    gather = Gather(shard, whole, sems) if share else None
    me = lax.axis_index("seq")
    half, wide = seq_ref.shape
    d = wide // 2
    step = wbuf.shape[2]
    chunks = d // step
    has_low = me > 0
    has_high = me < count - 1
    low_id = {"seq": lax.rem(me + count - 1, count)}
    high_id = {"seq": lax.rem(me + 1, count)}

    def w_copy(c):
        return pltpu.make_async_copy(w_ref.at[:, pl.ds(c * step, step)], wbuf.at[c], w_sem.at[c])

    for c in range(chunks):
        w_copy(c).start()

    barrier = pltpu.get_barrier_semaphore()

    if share:
        for o in range(1, count):
            pl.semaphore_signal(
                barrier, inc=1, device_id={"seq": lax.rem(me + o, count)}, device_id_type=MESH)
        for o in range(1, DP):
            pl.semaphore_signal(
                barrier, inc=1, device_id={"dp": (gather.dp + o) % DP}, device_id_type=MESH)
        pl.semaphore_wait(barrier, count + DP - 2)
    else:
        for peer in (low_id, high_id):
            pl.semaphore_signal(barrier, inc=1, device_id=peer, device_id_type=MESH)
        pl.semaphore_wait(barrier, 2)

    up = pltpu.make_async_remote_copy(
        src_ref=seq_ref.at[pl.ds(half - HALO, HALO)], dst_ref=low,
        send_sem=send_sem.at[0], recv_sem=recv_sem.at[0], device_id=high_id, device_id_type=MESH)
    down = pltpu.make_async_remote_copy(
        src_ref=seq_ref.at[pl.ds(0, HALO)], dst_ref=high,
        send_sem=send_sem.at[1], recv_sem=recv_sem.at[1], device_id=low_id, device_id_type=MESH)

    @pl.when(has_high)
    def _():
        up.start()

    @pl.when(has_low)
    def _():
        down.start()

    if share:
        gather.start()

    def activate(rows):
        rows = rows.astype(jnp.float32)
        scale = lax.rsqrt(jnp.mean(rows * rows, axis=-1, keepdims=True) + 1e-06)
        return jax.nn.gelu(rows * scale)

    block = 32

    def act_step(i, _):
        r = pl.multiple_of(i * block, block)
        ebuf[pl.ds(r + 8, block), :] = activate(seq_ref[pl.ds(r, block), :d])
        obuf[pl.ds(r + 8, block), :] = activate(seq_ref[pl.ds(r, block), d:])
        return 0

    lax.fori_loop(0, half // block, act_step, 0)

    @pl.when(has_low)
    def _():
        down.wait_send()
        up.wait_recv()
        ebuf[0:8, :] = activate(low[:, :d])[8:16]
        obuf[0:8, :] = activate(low[:, d:])[8:16]

    @pl.when(jnp.logical_not(has_low))
    def _():
        ebuf[0:8, :] = jnp.zeros((8, d), jnp.float32)
        obuf[0:8, :] = jnp.zeros((8, d), jnp.float32)

    @pl.when(has_high)
    def _():
        up.wait_send()
        down.wait_recv()
        ebuf[half + 8 : half + 16, :] = activate(high[:, :d])[0:8]
        obuf[half + 8 : half + 16, :] = activate(high[:, d:])[0:8]

    @pl.when(jnp.logical_not(has_high))
    def _():
        ebuf[half + 8 : half + 16, :] = jnp.zeros((8, d), jnp.float32)
        obuf[half + 8 : half + 16, :] = jnp.zeros((8, d), jnp.float32)

    def place(c, _):
        k = pl.multiple_of(c * step, step)
        cols = pl.ds(k, step)

        def put(first, tap, value):
            taps[first : first + half, pl.ds(tap * d + k, step)] = value

        e_prev = ebuf[7 : 7 + half, cols].astype(jnp.bfloat16)
        e_here = ebuf[8 : 8 + half, cols].astype(jnp.bfloat16)
        e_next = ebuf[9 : 9 + half, cols].astype(jnp.bfloat16)
        put(0, 0, e_prev)
        put(0, 2, e_here)
        put(half, 1, e_here)
        put(0, 4, e_next)
        put(half, 3, e_next)
        o_prev = obuf[7 : 7 + half, cols].astype(jnp.bfloat16)
        o_here = obuf[8 : 8 + half, cols].astype(jnp.bfloat16)
        o_next = obuf[9 : 9 + half, cols].astype(jnp.bfloat16)
        put(0, 1, o_prev)
        put(half, 0, o_prev)
        put(0, 3, o_here)
        put(half, 2, o_here)
        put(half, 4, o_next)
        return 0

    lax.fori_loop(0, chunks, place, 0)

    def conv_step(c, _):
        if share:
            gather.relay(c)

            @pl.when(c >= LAG)
            def _():
                gather.second(c - LAG)

        w_copy(c).wait()
        k = pl.multiple_of(c * step, step)
        mixed = jnp.dot(taps[...], wbuf[c], preferred_element_type=jnp.float32)
        even = mixed[:half] + seq_ref[:, pl.ds(k, step)].astype(jnp.float32)
        odd = mixed[half:] + seq_ref[:, pl.ds(k + d, step)].astype(jnp.float32)
        pooled_ref[:, pl.ds(k, step)] = jnp.maximum(even, odd).astype(jnp.bfloat16)
        return 0

    lax.fori_loop(0, chunks, conv_step, 0)
    if share:
        gather.finish()


def conv_pool(sequence, conv_weight, count, shard=None):
    rows, d = sequence.shape
    half = rows // 2
    step = 256
    pairs = sequence.reshape(half, 2 * d)
    weight = conv_weight.reshape(WIDTH * d, d)
    share = shard is not None
    out_shape = jax.ShapeDtypeStruct((half, d), jnp.bfloat16)
    out_specs = pl.BlockSpec(memory_space=pltpu.VMEM)
    in_specs = [pl.BlockSpec(memory_space=pltpu.VMEM), pl.BlockSpec(memory_space=pl.ANY)]
    operands, sems = [pairs, weight], []
    if share:
        out_shape = (out_shape, jax.ShapeDtypeStruct((count,) + shard.shape, jnp.bfloat16))
        out_specs = (out_specs, pl.BlockSpec(memory_space=pl.ANY))
        in_specs.append(pl.BlockSpec(memory_space=pl.ANY))
        operands.append(shard)
        sems = [pltpu.SemaphoreType.DMA((count,))] * 2 + [pltpu.SemaphoreType.DMA((count, DP))] * 4
        sems.append(pltpu.SemaphoreType.DMA((1,)))
    return pl.pallas_call(
        functools.partial(conv_kernel, count, share),
        out_shape=out_shape,
        in_specs=in_specs,
        out_specs=out_specs,
        scratch_shapes=[
            pltpu.VMEM((HALO, 2 * d), jnp.bfloat16),
            pltpu.VMEM((HALO, 2 * d), jnp.bfloat16),
            pltpu.VMEM((d // step, WIDTH * d, step), jnp.bfloat16),
            pltpu.VMEM((half + 16, d), jnp.float32),
            pltpu.VMEM((half + 16, d), jnp.float32),
            pltpu.VMEM((rows, WIDTH * d), jnp.bfloat16),
            pltpu.SemaphoreType.DMA((2,)),
            pltpu.SemaphoreType.DMA((2,)),
            pltpu.SemaphoreType.DMA((d // step,)),
        ] + sems,
        compiler_params=pltpu.CompilerParams(
            collective_id=0, has_side_effects=True, vmem_limit_bytes=52 * MB),
        cost_estimate=pl.CostEstimate(
            flops=2 * rows * WIDTH * d * d, bytes_accessed=2 * WIDTH * d * d, transcendentals=rows * d),
        name="conv_pool",
    )(*operands)


def attend_kernel(pooled_ref, w_ref, update_ref, normed, wbuf, owbuf, send, recv, att_send, att_recv,
                  send_sem, recv_sem, asend_sem, arecv_sem, w_sem):
    me = lax.axis_index("seq")
    count, d = pooled_ref.shape
    inner = HEADS * HEAD_DIM
    depth = d // HEADS

    def w_copy(t):
        return pltpu.make_async_copy(
            w_ref.at[:, pl.ds(0, depth), pl.ds(t * inner, inner)], wbuf.at[t], w_sem.at[t])

    def ow_copy(part):
        return pltpu.make_async_copy(
            w_ref.at[:, pl.ds(depth, HEAD_DIM // 2), pl.ds(part * d, d)], owbuf.at[:, part], w_sem.at[3 + part])

    order = (1, 2, 0)
    for t in order:
        w_copy(t).start()
    for part in range(2):
        ow_copy(part).start()

    barrier = pltpu.get_barrier_semaphore()

    def greet(o, _):
        pl.semaphore_signal(
            barrier, inc=1, device_id={"seq": lax.rem(me + o, HEADS)}, device_id_type=MESH)
        return 0

    lax.fori_loop(1, HEADS, greet, 0)

    def norm_step(i, _):
        r = pl.multiple_of(i * 32, 32)
        rows = pooled_ref[pl.ds(r, 32), :].astype(jnp.float32)
        scale = lax.rsqrt(jnp.mean(rows * rows, axis=-1, keepdims=True) + 1e-06)
        normed[pl.ds(r, 32), :] = (rows * scale).astype(jnp.bfloat16)
        return 0

    lax.fori_loop(0, count // 32, norm_step, 0)
    pl.semaphore_wait(barrier, HEADS - 1)

    def piece(t, peer, slot):
        return pltpu.make_async_remote_copy(
            src_ref=send.at[t, peer], dst_ref=recv.at[t, slot],
            send_sem=send_sem.at[t, peer], recv_sem=recv_sem.at[t, slot],
            device_id={"seq": peer}, device_id_type=MESH)

    def back(peer, slot):
        return pltpu.make_async_remote_copy(
            src_ref=att_send.at[peer], dst_ref=att_recv.at[slot],
            send_sem=asend_sem.at[peer], recv_sem=arecv_sem.at[slot],
            device_id={"seq": peer}, device_id_type=MESH)

    for t in order:
        w_copy(t).wait()

        def project(p, _, t=t):
            k = pl.multiple_of(p * 256, 256)
            both = jnp.dot(
                normed[...], wbuf[t, :, :, pl.ds(k, 256)].reshape(d, 256), preferred_element_type=jnp.float32
            ).astype(jnp.bfloat16)
            send[t, 2 * p] = both[:, :HEAD_DIM]
            send[t, 2 * p + 1] = both[:, HEAD_DIM:]
            return 0

        lax.fori_loop(0, HEADS // 2, project, 0)

        def post(o, _, t=t):
            piece(t, lax.rem(me + o, HEADS), me).start()
            return 0

        lax.fori_loop(1, HEADS, post, 0)
        recv[t, me] = send[t, me]

    def arrive(t):
        def one(o, _):
            source = lax.rem(me + HEADS - o, HEADS)
            piece(t, source, source).wait_recv()
            return 0

        lax.fori_loop(1, HEADS, one, 0)

    arrive(1)
    arrive(2)
    keys = recv.at[1]
    values = recv.at[2]
    factor = HEAD_DIM ** (-0.5) * 1.4426950408889634

    def attend(source):
        total_rows = HEADS * count
        raw = lax.dot_general(
            recv[0, source], keys[...].reshape(total_rows, HEAD_DIM),
            (((1,), (1,)), ((), ())), preferred_element_type=jnp.float32)
        peak = jnp.max(raw, axis=-1, keepdims=True)
        expo = jnp.exp2((raw - peak) * factor)
        total = jnp.sum(expo, axis=-1, keepdims=True)
        weighted = jnp.dot(
            expo.astype(jnp.bfloat16), values[...].reshape(total_rows, HEAD_DIM),
            preferred_element_type=jnp.float32)
        return (weighted / total).astype(jnp.bfloat16)

    def step(o, _):
        source = lax.rem(me + HEADS - o, HEADS)

        @pl.when(o > 0)
        def _():
            piece(0, source, source).wait_recv()

        att_send[source] = attend(source)

        @pl.when(o > 0)
        def _():
            back(source, me).start()

        return 0

    lax.fori_loop(0, HEADS, step, 0)
    att_recv[me] = att_send[me]

    def finish(o, _):
        peer = lax.rem(me + o, HEADS)
        for t in range(3):
            piece(t, peer, me).wait_send()
        back(peer, me).wait_send()
        back(peer, peer).wait_recv()
        return 0

    lax.fori_loop(1, HEADS, finish, 0)
    for part in range(2):
        ow_copy(part).wait()
    joined = jnp.concatenate([att_recv[h] for h in range(HEADS)], axis=1)
    for p in range(d // 512):
        update_ref[:, p * 512 : (p + 1) * 512] = jnp.dot(
            joined, owbuf[:, :, :, p * 512 : (p + 1) * 512].reshape(inner, 512), preferred_element_type=jnp.float32
        ).astype(jnp.bfloat16)


def attention(pooled, weights):
    count, d = pooled.shape
    inner = HEADS * HEAD_DIM
    heads = (HEADS, count, HEAD_DIM)
    return pl.pallas_call(
        attend_kernel,
        out_shape=jax.ShapeDtypeStruct((count, d), jnp.bfloat16),
        in_specs=[
            pl.BlockSpec(memory_space=pltpu.VMEM),
            pl.BlockSpec(memory_space=pl.ANY),
        ],
        out_specs=pl.BlockSpec(memory_space=pltpu.VMEM),
        scratch_shapes=[
            pltpu.VMEM((count, d), jnp.bfloat16),
            pltpu.VMEM((3, HEADS, d // HEADS, inner), jnp.bfloat16),
            pltpu.VMEM((HEADS, 2, HEAD_DIM // 2, d), jnp.bfloat16),
            pltpu.VMEM((3,) + heads, jnp.bfloat16),
            pltpu.VMEM((3,) + heads, jnp.bfloat16),
            pltpu.VMEM(heads, jnp.bfloat16),
            pltpu.VMEM(heads, jnp.bfloat16),
            pltpu.SemaphoreType.DMA((3, HEADS)),
            pltpu.SemaphoreType.DMA((3, HEADS)),
            pltpu.SemaphoreType.DMA((HEADS,)),
            pltpu.SemaphoreType.DMA((HEADS,)),
            pltpu.SemaphoreType.DMA((5,)),
        ],
        compiler_params=pltpu.CompilerParams(
            collective_id=1, has_side_effects=True, vmem_limit_bytes=44 * MB),
        cost_estimate=pl.CostEstimate(
            flops=2 * count * d * 4 * inner + 4 * count * HEADS * count * inner,
            bytes_accessed=8 * d * inner, transcendentals=count * count * HEADS * HEADS),
        name="attend",
    )(pooled, weights)


def normalize(values):
    return values * lax.rsqrt(jnp.mean(values * values, axis=-1, keepdims=True) + 1e-06)


def single_head(triple):
    query_rows, key_rows, value_rows = triple
    scores = jnp.dot(query_rows, key_rows.T, preferred_element_type=jnp.float32) * HEAD_DIM ** (
        -0.5
    )
    peak = jnp.max(scores, axis=-1, keepdims=True)
    expo = jnp.exp(scores - peak)
    total = jnp.sum(expo, axis=-1, keepdims=True)
    return (
        jnp.dot(expo.astype(jnp.bfloat16), value_rows, preferred_element_type=jnp.float32) / total
    ).astype(jnp.bfloat16)


def attention_groups(pooled, qkv_weight, out_weight):
    inner = HEADS * HEAD_DIM
    count = pooled.shape[0]
    normed = normalize(pooled.astype(jnp.float32)).astype(jnp.bfloat16)
    projected = jnp.dot(
        normed,
        lax.all_gather(qkv_weight, "seq", axis=0, tiled=True),
        preferred_element_type=jnp.float32,
    ).astype(jnp.bfloat16)
    seq_count = lax.axis_size("seq")
    groups = seq_count // HEADS
    share = count // groups
    query_send = (
        projected[:, :inner]
        .reshape(groups, share, HEADS, HEAD_DIM)
        .transpose(2, 0, 1, 3)
        .reshape(seq_count, share, HEAD_DIM)
    )
    pair_send = (
        projected[:, inner:]
        .reshape(count, 2, HEADS, HEAD_DIM)
        .transpose(2, 0, 1, 3)
        .reshape(HEADS, count, 2 * HEAD_DIM)
    )
    pair_send = jnp.repeat(pair_send, groups, axis=0)
    query_recv, pair_recv = (
        lax.all_to_all(query_send, "seq", split_axis=0, concat_axis=0, tiled=True),
        lax.all_to_all(pair_send, "seq", split_axis=0, concat_axis=0, tiled=True),
    )
    key_rows = pair_recv[:, :, :HEAD_DIM].reshape(seq_count * count, HEAD_DIM)
    value_rows = pair_recv[:, :, HEAD_DIM:].reshape(seq_count * count, HEAD_DIM)

    def per_source(query_rows):
        return single_head((query_rows, key_rows, value_rows))

    head_rows = lax.map(per_source, query_recv)
    returned = lax.all_to_all(head_rows, "seq", split_axis=0, concat_axis=0, tiled=True)
    attended = (
        returned.reshape(HEADS, groups, share, HEAD_DIM).transpose(1, 2, 0, 3).reshape(count, inner)
    )
    columns = attended
    update = jnp.dot(
        columns,
        lax.all_gather(out_weight, "seq", axis=0, tiled=True),
        preferred_element_type=jnp.float32,
    )
    return update.astype(jnp.bfloat16)


def on_device(sequence, conv_weight, qkv_weight, out_weight):
    count = lax.axis_size("seq")
    if count == HEADS and lax.axis_size("dp") == DP:
        part = out_weight.shape[0] // 2
        shard = jnp.concatenate(
            [qkv_weight, jnp.concatenate([out_weight[:part], out_weight[part:]], axis=1)], axis=0)
        pooled, weights = conv_pool(sequence, conv_weight, count, shard)
        update = attention(pooled, weights)
    else:
        pooled = conv_pool(sequence, conv_weight, count)
        update = attention_groups(pooled, qkv_weight, out_weight)
    return (pooled, update)


def solution(mesh):
    return jax.shard_map(
        on_device,
        mesh=mesh,
        in_specs=(P(("dp", "seq"), None), P(), P("seq", None), P("seq", None)),
        out_specs=(P(("dp", "seq"), None), P(("dp", "seq"), None)),
        check_vma=False,
    )
```

```python
import functools

import jax
import jax.numpy as jnp
from jax import lax
from jax.experimental import pallas as pl
from jax.experimental.pallas import tpu as pltpu
from jax.sharding import PartitionSpec as P

HEADS = 8
HEAD_DIM = 128
WIDTH = 5
MESH = pl.DeviceIdType.MESH
HALO = 16
MB = 1024 * 1024
DP = 4
PAIRS = 4
REMOTE = 6
WINDOW = 2
LAG = 2


class Gather:
    def __init__(self, first, second, whole, sems):
        self.first, self.last, self.whole = first, second, whole
        self.s1, self.r1, self.s2, self.r2, self.s3, self.r3, self.s4, self.own_sem = sems
        self.me = lax.axis_index("seq")
        self.dp = lax.axis_index("dp")
        self.pair, self.core = self.me // 2, self.me % 2
        self.mate = self.pair * 2 + 1 - self.core
        self.shard = whole.at[self.me]
        self.mates = (self.dp, self.dp + 1 - 2 * (self.dp % 2), (self.dp + 2) % DP, DP - 1 - self.dp)
        self.width = whole.shape[1] // (2 * DP)

    def part(self, source, group, core):
        first = pl.multiple_of((2 * group + core) * self.width, self.width)
        return self.whole.at[source, pl.ds(first, self.width)]

    def own(self):
        depth, wide = self.first.shape
        part = self.last.shape[0] // 2
        copies = [pltpu.make_async_copy(self.first, self.shard.at[pl.ds(0, depth)], self.own_sem.at[0])]
        for k in range(2):
            copies.append(pltpu.make_async_copy(
                self.last.at[pl.ds(k * part, part)],
                self.shard.at[pl.ds(depth, part), pl.ds(k * wide // 2, wide // 2)], self.own_sem.at[k + 1]))
        return copies

    def to_mate(self):
        return pltpu.make_async_remote_copy(
            src_ref=self.shard, dst_ref=self.whole.at[self.me], send_sem=self.s1.at[self.mate],
            recv_sem=self.r1.at[self.me], device_id={"seq": self.mate}, device_id_type=MESH)

    def from_mate(self):
        return pltpu.make_async_remote_copy(
            src_ref=self.shard, dst_ref=self.whole.at[self.mate], send_sem=self.s1.at[self.me],
            recv_sem=self.r1.at[self.mate], device_id={"seq": self.mate}, device_id_type=MESH)

    def target(self, i):
        return ((self.pair + PAIRS - 1 - i // 2) % PAIRS) * 2 + i % 2

    def source(self, i):
        return ((self.pair + 1 + i // 2) % PAIRS) * 2 + i % 2

    def out1(self, i):
        peer = self.target(i)
        first = pl.multiple_of((2 * self.dp + peer % 2) * self.width, self.width)
        return pltpu.make_async_remote_copy(
            src_ref=self.shard.at[pl.ds(first, self.width)], dst_ref=self.part(self.me, self.dp, peer % 2),
            send_sem=self.s1.at[peer], recv_sem=self.r1.at[self.me], device_id={"seq": peer}, device_id_type=MESH)

    def out4(self, i):
        peer, group = self.target(i), self.mates[3]
        block = self.part(self.me, group, peer % 2)
        return pltpu.make_async_remote_copy(
            src_ref=block, dst_ref=block, send_sem=self.s4.at[peer], recv_sem=self.r2.at[self.me, group],
            device_id={"seq": peer}, device_id_type=MESH)

    def in1(self, i):
        source = self.source(i)
        block = self.part(source, self.dp, self.core)
        return pltpu.make_async_remote_copy(
            src_ref=block, dst_ref=block, send_sem=self.s1.at[source], recv_sem=self.r1.at[source],
            device_id={"seq": source}, device_id_type=MESH)

    def out2(self, i, j):
        source, peer = self.source(i), self.mates[j]
        block = self.part(source, self.dp, self.core)
        return pltpu.make_async_remote_copy(
            src_ref=block, dst_ref=block, send_sem=self.s2.at[source, peer], recv_sem=self.r2.at[source, self.dp],
            device_id={"dp": peer}, device_id_type=MESH)

    def in2(self, i, j):
        source, peer = self.source(i), self.mates[j]
        block = self.part(source, peer, self.core)
        return pltpu.make_async_remote_copy(
            src_ref=block, dst_ref=block, send_sem=self.s2.at[source, peer], recv_sem=self.r2.at[source, peer],
            device_id={"dp": peer}, device_id_type=MESH)

    def out3(self, i, group):
        source = self.source(i)
        block = self.part(source, group, self.core)
        return pltpu.make_async_remote_copy(
            src_ref=block, dst_ref=block, send_sem=self.s3.at[source, group], recv_sem=self.r3.at[source, group],
            device_id={"seq": self.mate}, device_id_type=MESH)

    def in3(self, i, group):
        source = self.source(i)
        block = self.part(source, group, 1 - self.core)
        return pltpu.make_async_remote_copy(
            src_ref=block, dst_ref=block, send_sem=self.s3.at[source, group], recv_sem=self.r3.at[source, group],
            device_id={"seq": self.mate}, device_id_type=MESH)

    def start(self):
        for copy in self.own():
            copy.wait()
        self.to_mate().start()

        def one(i, _):
            self.out1(i).start()
            return 0


        lax.fori_loop(0, WINDOW, one, 0)

    def relay(self, i):
        self.out1(i).wait_send()

        @pl.when(i + WINDOW < REMOTE)
        def _():
            self.out1(i + WINDOW).start()

        self.in1(i).wait_recv()
        for j in range(1, DP - 1):
            self.out2(i, j).start()

        @pl.when(self.core == 0)
        def _():
            self.out4(i).start()

        @pl.when(i % 2 == 1)
        def _():
            self.out2(i, DP - 1).start()

        self.out3(i, self.dp).start()

    def second(self, i):
        for j in range(1, DP):
            self.in2(i, j).wait_recv()
            self.out3(i, self.mates[j]).start()

    def finish(self):
        def rest(i, _):
            self.second(i)
            return 0

        lax.fori_loop(REMOTE - LAG, REMOTE, rest, 0)

        def last(i, _):
            for j in range(1, DP - 1):
                self.out2(i, j).wait_send()

            @pl.when(self.core == 0)
            def _():
                self.out4(i).wait_send()

            @pl.when(i % 2 == 1)
            def _():
                self.out2(i, DP - 1).wait_send()

            for group in range(DP):
                self.out3(i, group).wait_send()
                self.in3(i, group).wait_recv()
            return 0

        lax.fori_loop(0, REMOTE, last, 0)
        self.to_mate().wait_send()
        self.from_mate().wait_recv()


def conv_kernel(count, share, *refs):
    if share:
        seq_ref, w_ref, first, second, pooled_ref, whole, *refs = refs
    else:
        seq_ref, w_ref, pooled_ref, *refs = refs
    low, high, wbuf, ebuf, obuf, taps, send_sem, recv_sem, w_sem, *sems = refs
    gather = Gather(first, second, whole, sems) if share else None
    if share:
        for copy in gather.own():
            copy.start()
    me = lax.axis_index("seq")
    half, wide = seq_ref.shape
    d = wide // 2
    step = wbuf.shape[2]
    chunks = d // step
    has_low = me > 0
    has_high = me < count - 1
    low_id = {"seq": lax.rem(me + count - 1, count)}
    high_id = {"seq": lax.rem(me + 1, count)}

    def w_copy(c):
        return pltpu.make_async_copy(w_ref.at[:, pl.ds(c * step, step)], wbuf.at[c], w_sem.at[c])

    for c in range(chunks):
        w_copy(c).start()

    barrier = pltpu.get_barrier_semaphore()

    if share:
        for o in range(1, count):
            pl.semaphore_signal(
                barrier, inc=1, device_id={"seq": lax.rem(me + o, count)}, device_id_type=MESH)
        for o in range(1, DP):
            pl.semaphore_signal(
                barrier, inc=1, device_id={"dp": (gather.dp + o) % DP}, device_id_type=MESH)
        pl.semaphore_wait(barrier, count + DP - 2)
    else:
        for peer in (low_id, high_id):
            pl.semaphore_signal(barrier, inc=1, device_id=peer, device_id_type=MESH)
        pl.semaphore_wait(barrier, 2)

    up = pltpu.make_async_remote_copy(
        src_ref=seq_ref.at[pl.ds(half - HALO, HALO)], dst_ref=low,
        send_sem=send_sem.at[0], recv_sem=recv_sem.at[0], device_id=high_id, device_id_type=MESH)
    down = pltpu.make_async_remote_copy(
        src_ref=seq_ref.at[pl.ds(0, HALO)], dst_ref=high,
        send_sem=send_sem.at[1], recv_sem=recv_sem.at[1], device_id=low_id, device_id_type=MESH)

    @pl.when(has_high)
    def _():
        up.start()

    @pl.when(has_low)
    def _():
        down.start()

    if share:
        gather.start()

    def activate(rows):
        rows = rows.astype(jnp.float32)
        scale = lax.rsqrt(jnp.mean(rows * rows, axis=-1, keepdims=True) + 1e-06)
        return jax.nn.gelu(rows * scale)

    block = 32

    def act_step(i, _):
        r = pl.multiple_of(i * block, block)
        ebuf[pl.ds(r + 8, block), :] = activate(seq_ref[pl.ds(r, block), :d])
        obuf[pl.ds(r + 8, block), :] = activate(seq_ref[pl.ds(r, block), d:])
        return 0

    lax.fori_loop(0, half // block, act_step, 0)

    @pl.when(has_low)
    def _():
        down.wait_send()
        up.wait_recv()
        ebuf[0:8, :] = activate(low[:, :d])[8:16]
        obuf[0:8, :] = activate(low[:, d:])[8:16]

    @pl.when(jnp.logical_not(has_low))
    def _():
        ebuf[0:8, :] = jnp.zeros((8, d), jnp.float32)
        obuf[0:8, :] = jnp.zeros((8, d), jnp.float32)

    @pl.when(has_high)
    def _():
        up.wait_send()
        down.wait_recv()
        ebuf[half + 8 : half + 16, :] = activate(high[:, :d])[0:8]
        obuf[half + 8 : half + 16, :] = activate(high[:, d:])[0:8]

    @pl.when(jnp.logical_not(has_high))
    def _():
        ebuf[half + 8 : half + 16, :] = jnp.zeros((8, d), jnp.float32)
        obuf[half + 8 : half + 16, :] = jnp.zeros((8, d), jnp.float32)

    def place(c, _):
        k = pl.multiple_of(c * step, step)
        cols = pl.ds(k, step)

        def put(first, tap, value):
            taps[first : first + half, pl.ds(tap * d + k, step)] = value

        e_prev = ebuf[7 : 7 + half, cols].astype(jnp.bfloat16)
        e_here = ebuf[8 : 8 + half, cols].astype(jnp.bfloat16)
        e_next = ebuf[9 : 9 + half, cols].astype(jnp.bfloat16)
        put(0, 0, e_prev)
        put(0, 2, e_here)
        put(half, 1, e_here)
        put(0, 4, e_next)
        put(half, 3, e_next)
        o_prev = obuf[7 : 7 + half, cols].astype(jnp.bfloat16)
        o_here = obuf[8 : 8 + half, cols].astype(jnp.bfloat16)
        o_next = obuf[9 : 9 + half, cols].astype(jnp.bfloat16)
        put(0, 1, o_prev)
        put(half, 0, o_prev)
        put(0, 3, o_here)
        put(half, 2, o_here)
        put(half, 4, o_next)
        return 0

    lax.fori_loop(0, chunks, place, 0)

    def conv_step(c, _):
        if share:
            gather.relay(c)

            @pl.when(c >= LAG)
            def _():
                gather.second(c - LAG)

        w_copy(c).wait()
        k = pl.multiple_of(c * step, step)
        mixed = jnp.dot(taps[...], wbuf[c], preferred_element_type=jnp.float32)
        even = mixed[:half] + seq_ref[:, pl.ds(k, step)].astype(jnp.float32)
        odd = mixed[half:] + seq_ref[:, pl.ds(k + d, step)].astype(jnp.float32)
        pooled_ref[:, pl.ds(k, step)] = jnp.maximum(even, odd).astype(jnp.bfloat16)
        return 0

    lax.fori_loop(0, chunks, conv_step, 0)
    if share:
        gather.finish()


def conv_pool(sequence, conv_weight, count, shard=None):
    rows, d = sequence.shape
    half = rows // 2
    step = 256
    pairs = sequence.reshape(half, 2 * d)
    weight = conv_weight.reshape(WIDTH * d, d)
    share = shard is not None
    out_shape = jax.ShapeDtypeStruct((half, d), jnp.bfloat16)
    out_specs = pl.BlockSpec(memory_space=pltpu.VMEM)
    in_specs = [pl.BlockSpec(memory_space=pltpu.VMEM), pl.BlockSpec(memory_space=pl.ANY)]
    operands, sems = [pairs, weight], []
    if share:
        out_shape = (out_shape, jax.ShapeDtypeStruct((count, shard[0].shape[0] + shard[1].shape[0] // 2, 2 * d), jnp.bfloat16))
        out_specs = (out_specs, pl.BlockSpec(memory_space=pl.ANY))
        in_specs += [pl.BlockSpec(memory_space=pl.ANY)] * 2
        operands += shard
        sems = [pltpu.SemaphoreType.DMA((count,))] * 2 + [pltpu.SemaphoreType.DMA((count, DP))] * 4
        sems += [pltpu.SemaphoreType.DMA((count,)), pltpu.SemaphoreType.DMA((3,))]
    return pl.pallas_call(
        functools.partial(conv_kernel, count, share),
        out_shape=out_shape,
        in_specs=in_specs,
        out_specs=out_specs,
        scratch_shapes=[
            pltpu.VMEM((HALO, 2 * d), jnp.bfloat16),
            pltpu.VMEM((HALO, 2 * d), jnp.bfloat16),
            pltpu.VMEM((d // step, WIDTH * d, step), jnp.bfloat16),
            pltpu.VMEM((half + 16, d), jnp.float32),
            pltpu.VMEM((half + 16, d), jnp.float32),
            pltpu.VMEM((rows, WIDTH * d), jnp.bfloat16),
            pltpu.SemaphoreType.DMA((2,)),
            pltpu.SemaphoreType.DMA((2,)),
            pltpu.SemaphoreType.DMA((d // step,)),
        ] + sems,
        compiler_params=pltpu.CompilerParams(
            collective_id=0, has_side_effects=True, vmem_limit_bytes=52 * MB),
        cost_estimate=pl.CostEstimate(
            flops=2 * rows * WIDTH * d * d, bytes_accessed=2 * WIDTH * d * d, transcendentals=rows * d),
        name="conv_pool",
    )(*operands)


def attend_kernel(pooled_ref, w_ref, update_ref, normed, wbuf, owbuf, send, recv, att_send, att_recv,
                  send_sem, recv_sem, asend_sem, arecv_sem, w_sem):
    me = lax.axis_index("seq")
    count, d = pooled_ref.shape
    inner = HEADS * HEAD_DIM
    depth = d // HEADS

    def w_copy(t):
        return pltpu.make_async_copy(
            w_ref.at[:, pl.ds(0, depth), pl.ds(t * inner, inner)], wbuf.at[t], w_sem.at[t])

    def ow_copy(part):
        return pltpu.make_async_copy(
            w_ref.at[:, pl.ds(depth, HEAD_DIM // 2), pl.ds(part * d, d)], owbuf.at[:, part], w_sem.at[3 + part])

    order = (1, 2, 0)
    for t in order:
        w_copy(t).start()
    for part in range(2):
        ow_copy(part).start()

    barrier = pltpu.get_barrier_semaphore()

    def greet(o, _):
        pl.semaphore_signal(
            barrier, inc=1, device_id={"seq": lax.rem(me + o, HEADS)}, device_id_type=MESH)
        return 0

    lax.fori_loop(1, HEADS, greet, 0)

    def norm_step(i, _):
        r = pl.multiple_of(i * 32, 32)
        rows = pooled_ref[pl.ds(r, 32), :].astype(jnp.float32)
        scale = lax.rsqrt(jnp.mean(rows * rows, axis=-1, keepdims=True) + 1e-06)
        normed[pl.ds(r, 32), :] = (rows * scale).astype(jnp.bfloat16)
        return 0

    lax.fori_loop(0, count // 32, norm_step, 0)
    pl.semaphore_wait(barrier, HEADS - 1)

    def piece(t, peer, slot):
        return pltpu.make_async_remote_copy(
            src_ref=send.at[t, peer], dst_ref=recv.at[t, slot],
            send_sem=send_sem.at[t, peer], recv_sem=recv_sem.at[t, slot],
            device_id={"seq": peer}, device_id_type=MESH)

    def back(peer, slot):
        return pltpu.make_async_remote_copy(
            src_ref=att_send.at[peer], dst_ref=att_recv.at[slot],
            send_sem=asend_sem.at[peer], recv_sem=arecv_sem.at[slot],
            device_id={"seq": peer}, device_id_type=MESH)

    for t in order:
        w_copy(t).wait()

        def project(p, _, t=t):
            k = pl.multiple_of(p * 256, 256)
            both = jnp.dot(
                normed[...], wbuf[t, :, :, pl.ds(k, 256)].reshape(d, 256), preferred_element_type=jnp.float32
            ).astype(jnp.bfloat16)
            send[t, 2 * p] = both[:, :HEAD_DIM]
            send[t, 2 * p + 1] = both[:, HEAD_DIM:]
            return 0

        lax.fori_loop(0, HEADS // 2, project, 0)

        def post(o, _, t=t):
            piece(t, lax.rem(me + o, HEADS), me).start()
            return 0

        lax.fori_loop(1, HEADS, post, 0)
        recv[t, me] = send[t, me]

    def arrive(t):
        def one(o, _):
            source = lax.rem(me + HEADS - o, HEADS)
            piece(t, source, source).wait_recv()
            return 0

        lax.fori_loop(1, HEADS, one, 0)

    arrive(1)
    arrive(2)
    keys = recv.at[1]
    values = recv.at[2]
    factor = HEAD_DIM ** (-0.5) * 1.4426950408889634

    def attend(source):
        total_rows = HEADS * count
        raw = lax.dot_general(
            recv[0, source], keys[...].reshape(total_rows, HEAD_DIM),
            (((1,), (1,)), ((), ())), preferred_element_type=jnp.float32)
        peak = jnp.max(raw, axis=-1, keepdims=True)
        expo = jnp.exp2((raw - peak) * factor)
        total = jnp.sum(expo, axis=-1, keepdims=True)
        weighted = jnp.dot(
            expo.astype(jnp.bfloat16), values[...].reshape(total_rows, HEAD_DIM),
            preferred_element_type=jnp.float32)
        return (weighted / total).astype(jnp.bfloat16)

    def step(o, _):
        source = lax.rem(me + HEADS - o, HEADS)

        @pl.when(o > 0)
        def _():
            piece(0, source, source).wait_recv()

        att_send[source] = attend(source)

        @pl.when(o > 0)
        def _():
            back(source, me).start()

        return 0

    lax.fori_loop(0, HEADS, step, 0)
    att_recv[me] = att_send[me]

    def finish(o, _):
        peer = lax.rem(me + o, HEADS)
        for t in range(3):
            piece(t, peer, me).wait_send()
        back(peer, me).wait_send()
        back(peer, peer).wait_recv()
        return 0

    lax.fori_loop(1, HEADS, finish, 0)
    for part in range(2):
        ow_copy(part).wait()
    joined = jnp.concatenate([att_recv[h] for h in range(HEADS)], axis=1)
    for p in range(d // 512):
        update_ref[:, p * 512 : (p + 1) * 512] = jnp.dot(
            joined, owbuf[:, :, :, p * 512 : (p + 1) * 512].reshape(inner, 512), preferred_element_type=jnp.float32
        ).astype(jnp.bfloat16)


def attention(pooled, weights):
    count, d = pooled.shape
    inner = HEADS * HEAD_DIM
    heads = (HEADS, count, HEAD_DIM)
    return pl.pallas_call(
        attend_kernel,
        out_shape=jax.ShapeDtypeStruct((count, d), jnp.bfloat16),
        in_specs=[
            pl.BlockSpec(memory_space=pltpu.VMEM),
            pl.BlockSpec(memory_space=pl.ANY),
        ],
        out_specs=pl.BlockSpec(memory_space=pltpu.VMEM),
        scratch_shapes=[
            pltpu.VMEM((count, d), jnp.bfloat16),
            pltpu.VMEM((3, HEADS, d // HEADS, inner), jnp.bfloat16),
            pltpu.VMEM((HEADS, 2, HEAD_DIM // 2, d), jnp.bfloat16),
            pltpu.VMEM((3,) + heads, jnp.bfloat16),
            pltpu.VMEM((3,) + heads, jnp.bfloat16),
            pltpu.VMEM(heads, jnp.bfloat16),
            pltpu.VMEM(heads, jnp.bfloat16),
            pltpu.SemaphoreType.DMA((3, HEADS)),
            pltpu.SemaphoreType.DMA((3, HEADS)),
            pltpu.SemaphoreType.DMA((HEADS,)),
            pltpu.SemaphoreType.DMA((HEADS,)),
            pltpu.SemaphoreType.DMA((5,)),
        ],
        compiler_params=pltpu.CompilerParams(
            collective_id=1, has_side_effects=True, vmem_limit_bytes=44 * MB),
        cost_estimate=pl.CostEstimate(
            flops=2 * count * d * 4 * inner + 4 * count * HEADS * count * inner,
            bytes_accessed=8 * d * inner, transcendentals=count * count * HEADS * HEADS),
        name="attend",
    )(pooled, weights)


def normalize(values):
    return values * lax.rsqrt(jnp.mean(values * values, axis=-1, keepdims=True) + 1e-06)


def single_head(triple):
    query_rows, key_rows, value_rows = triple
    scores = jnp.dot(query_rows, key_rows.T, preferred_element_type=jnp.float32) * HEAD_DIM ** (
        -0.5
    )
    peak = jnp.max(scores, axis=-1, keepdims=True)
    expo = jnp.exp(scores - peak)
    total = jnp.sum(expo, axis=-1, keepdims=True)
    return (
        jnp.dot(expo.astype(jnp.bfloat16), value_rows, preferred_element_type=jnp.float32) / total
    ).astype(jnp.bfloat16)


def attention_groups(pooled, qkv_weight, out_weight):
    inner = HEADS * HEAD_DIM
    count = pooled.shape[0]
    normed = normalize(pooled.astype(jnp.float32)).astype(jnp.bfloat16)
    projected = jnp.dot(
        normed,
        lax.all_gather(qkv_weight, "seq", axis=0, tiled=True),
        preferred_element_type=jnp.float32,
    ).astype(jnp.bfloat16)
    seq_count = lax.axis_size("seq")
    groups = seq_count // HEADS
    share = count // groups
    query_send = (
        projected[:, :inner]
        .reshape(groups, share, HEADS, HEAD_DIM)
        .transpose(2, 0, 1, 3)
        .reshape(seq_count, share, HEAD_DIM)
    )
    pair_send = (
        projected[:, inner:]
        .reshape(count, 2, HEADS, HEAD_DIM)
        .transpose(2, 0, 1, 3)
        .reshape(HEADS, count, 2 * HEAD_DIM)
    )
    pair_send = jnp.repeat(pair_send, groups, axis=0)
    query_recv, pair_recv = (
        lax.all_to_all(query_send, "seq", split_axis=0, concat_axis=0, tiled=True),
        lax.all_to_all(pair_send, "seq", split_axis=0, concat_axis=0, tiled=True),
    )
    key_rows = pair_recv[:, :, :HEAD_DIM].reshape(seq_count * count, HEAD_DIM)
    value_rows = pair_recv[:, :, HEAD_DIM:].reshape(seq_count * count, HEAD_DIM)

    def per_source(query_rows):
        return single_head((query_rows, key_rows, value_rows))

    head_rows = lax.map(per_source, query_recv)
    returned = lax.all_to_all(head_rows, "seq", split_axis=0, concat_axis=0, tiled=True)
    attended = (
        returned.reshape(HEADS, groups, share, HEAD_DIM).transpose(1, 2, 0, 3).reshape(count, inner)
    )
    columns = attended
    update = jnp.dot(
        columns,
        lax.all_gather(out_weight, "seq", axis=0, tiled=True),
        preferred_element_type=jnp.float32,
    )
    return update.astype(jnp.bfloat16)


def on_device(sequence, conv_weight, qkv_weight, out_weight):
    count = lax.axis_size("seq")
    if count == HEADS and lax.axis_size("dp") == DP:
        pooled, weights = conv_pool(sequence, conv_weight, count, [qkv_weight, out_weight])
        update = attention(pooled, weights)
    else:
        pooled = conv_pool(sequence, conv_weight, count)
        update = attention_groups(pooled, qkv_weight, out_weight)
    return (pooled, update)


def solution(mesh):
    return jax.shard_map(
        on_device,
        mesh=mesh,
        in_specs=(P(("dp", "seq"), None), P(), P("seq", None), P("seq", None)),
        out_specs=(P(("dp", "seq"), None), P(("dp", "seq"), None)),
        check_vma=False,
    )
```
